32 devices in a mesh: groups: 2 (over x), tm: 16 (over z, y, core).
Axes of the slice: x: 2, y: 2, z: 4, core: 2. Of those that a mesh axis runs over, the one named last changes fastest.
Arguments:
- velocity: bfloat16 [16, 4, 2, 32, 512], P('tm', None, None, 'groups'), parts along dimension 3, may hold values from -0.29882812 to 0.29882812
- substep_count: int32 [16], P('tm'), may hold values from 9 to 12
- sea_mask: int32 [32, 512], P('groups'), parts along dimension 0, may hold values 0 or 1
Outputs:
- forward_strain: float32 [16, 3, 32, 512], P('tm', None, 'groups'), parts along dimension 2
- backward_strain: float32 [16, 3, 32, 512], P('tm', None, 'groups'), parts along dimension 2
- forward_shift: float32 [16, 2, 32, 512], P('tm', None, 'groups'), parts along dimension 2
- backward_shift: float32 [16, 2, 32, 512], P('tm', None, 'groups'), parts along dimension 2
The draws below stay inside these ranges and needn't reach their ends.
There are 2 independent parts, one for each index of `groups`. The reference program is written for one: setup_inputs(seed, part) draws one part's arguments, and reference() takes and returns one part's arrays. A program takes and returns all parts, laid end to end along the dimension named above; an argument that names none is the same for every part. Nothing has to cross between parts.
All inputs are finite; a program needn't handle non-finite values.
Results may differ from the reference program's by a relative error of at most 0.0003.
Values sent between devices are 32-bit elements; how exact they have to be, the bound alone decides.
No kernel may reach another device: no remote copies, remote signals or barrier semaphores. Data moves between devices by JAX's collectives and lax.ppermute only.
A program may use at most 192 MiB of HBM per device.

```python
import jax
import jax.numpy as jnp
from jax import lax

RX = 16
RY = 512
SNAPS = 4
SUBSTEPS = 12
RADIUS = 4
WINDOWS = 16


def with_ends(values, stream_key, smallest, top_value):
    extent = values.shape
    spot = [jax.random.randint(jax.random.fold_in(stream_key, axis), (), 0, extent[axis]) for axis in range(len(extent))]
    values = values.at[tuple(spot)].set(smallest)
    longest = extent.index(max(extent))
    spot[longest] = (spot[longest] + 1) % extent[longest]
    return values.at[tuple(spot)].set(top_value)


def levels(stream_key, extent, pieces, least, top_value):
    gain = 1.0
    for axis_at, shards_of in pieces:
        steps = jax.random.uniform(jax.random.fold_in(jax.random.fold_in(stream_key, 6), axis_at), (shards_of,), jnp.float32, least / len(pieces), top_value / len(pieces))
        gain = gain * jnp.repeat(jnp.exp(steps), extent[axis_at] // shards_of).reshape((-1,) + (1,) * (len(extent) - 1 - axis_at))
    return gain


def scatter_about(key, shape, width, bound, cuts=(), dtype=jnp.bfloat16):
    factor_of = levels(key, shape, cuts, -0.22, 0.18) if cuts else 1.0
    array = jax.random.normal(key, shape, jnp.float32) * width * factor_of
    return jnp.minimum(jnp.maximum(array, -bound), bound).astype(dtype)


def setup_inputs(seed: int = 0, part: int = 0) -> dict:
    key_list = jax.random.split(jax.random.key(seed), 4)
    own_keys = jax.random.split(jax.random.fold_in(key_list[3], part), 4)
    velocity = scatter_about(own_keys[0], (WINDOWS, SNAPS, 2, RX, RY), 0.1, 0.29882812, ((0, 16),))
    substep_count = with_ends(jax.random.randint(key_list[1], (WINDOWS,), 9, 13), jax.random.fold_in(key_list[1], 1), 9, 12).astype(jnp.int32)
    sea_mask = with_ends((jax.random.randint(own_keys[2], (RX, RY), 0, 8) < 7).astype(jnp.int32), jax.random.fold_in(own_keys[2], 1), 0, 1)
    return {"velocity": velocity, "substep_count": substep_count, "sea_mask": sea_mask}


def stencil_tables(size):
    place = jnp.arange(size)
    offset = (place[None, :] - place[:, None]).astype(jnp.float32)
    hat = jnp.maximum(RADIUS + 1.0 - jnp.abs(offset), 0.0)
    spots = jnp.arange(-RADIUS, RADIUS + 1).astype(jnp.float32)
    weights = RADIUS + 1.0 - jnp.abs(spots)
    smooth = hat / jnp.sum(weights)
    slope = hat * offset / jnp.sum(weights * spots * spots)
    return smooth, slope


def window_map(vel, count, sea, sign, flipped):
    flow = vel.astype(jnp.float32) * sea.astype(jnp.float32)[None, None]
    if flipped:
        flow = flow[::-1]
    flow = sign * flow

    def advance(step, disp):
        snap = lax.dynamic_index_in_dim(flow, step // 3, 0, keepdims=False)
        upart = snap[0]
        vpart = snap[1]
        padded = jnp.pad(disp, ((0, 0), (1, 1), (1, 1)), mode="edge")
        back_x = disp - padded[:, :-2, 1:-1]
        fore_x = padded[:, 2:, 1:-1] - disp
        back_y = disp - padded[:, 1:-1, :-2]
        fore_y = padded[:, 1:-1, 2:] - disp
        tend = (jnp.maximum(upart, 0.0) * back_x + jnp.minimum(upart, 0.0) * fore_x
                + jnp.maximum(vpart, 0.0) * back_y + jnp.minimum(vpart, 0.0) * fore_y + snap)
        return jnp.where(step < count, disp - tend, disp)

    start = jnp.zeros(flow.shape[1:], jnp.float32)
    return lax.fori_loop(0, SUBSTEPS, advance, start)


def local_state(disp):
    smooth_x, slope_x = stencil_tables(disp.shape[1])
    smooth_y, slope_y = stencil_tables(disp.shape[2])
    high = lax.Precision.HIGHEST
    along_y = jnp.einsum("kab,cb->kac", disp, smooth_y, precision=high)
    grad_x = jnp.einsum("ra,kac->krc", slope_x, along_y, precision=high)
    across_y = jnp.einsum("kab,cb->kac", disp, slope_y, precision=high)
    grad_y = jnp.einsum("ra,kac->krc", smooth_x, across_y, precision=high)
    return jnp.stack([1.0 + grad_x[0], grad_y[0], grad_x[1], 1.0 + grad_y[1], disp[0], disp[1]], axis=0)


def join(first, then):
    e0, e1, e2, e3, e4, e5 = [first[..., k, :, :] for k in range(6)]
    l0, l1, l2, l3, l4, l5 = [then[..., k, :, :] for k in range(6)]
    return jnp.stack([l0 * e0 + l1 * e2, l0 * e1 + l1 * e3, l2 * e0 + l3 * e2, l2 * e1 + l3 * e3,
                      l4 + l0 * e4 + l1 * e5, l5 + l2 * e4 + l3 * e5], axis=-3)


def strain(state):
    a11, a12, a21, a22 = state[..., 0, :, :], state[..., 1, :, :], state[..., 2, :, :], state[..., 3, :, :]
    return jnp.stack([a11 * a11 + a21 * a21, a11 * a12 + a21 * a22, a12 * a12 + a22 * a22], axis=-3)


def reference(velocity, substep_count, sea_mask):
    def both(pair):
        vel, count = pair
        ahead = local_state(window_map(vel, count, sea_mask, -1.0, True))
        behind = local_state(window_map(vel, count, sea_mask, 1.0, False))
        return ahead, behind

    ahead_all, behind_all = lax.map(both, (velocity, substep_count))
    ident = jnp.zeros(ahead_all.shape[1:], jnp.float32).at[0].set(1.0).at[3].set(1.0)

    def compose(carry, own):
        total = join(carry, own)
        return total, total

    _, fwd = lax.scan(compose, ident, ahead_all)
    _, bwd = lax.scan(compose, ident, behind_all, reverse=True)
    return strain(fwd), strain(bwd), fwd[:, 4:6], bwd[:, 4:6]
```

```python
import functools

import jax
import jax.numpy as jnp
from jax import lax
from jax.experimental import pallas as pl
from jax.experimental.pallas import tpu as pltpu
from jax.sharding import PartitionSpec as P

SUBSTEPS = 12
RADIUS = 4
LANES = 128
F32 = jnp.float32
BF16 = jnp.bfloat16


def advance_kernel(count_ref, vel_ref, sea_ref, out_ref):
    snaps, _, rows, cols = vel_ref.shape[1:]
    per_snap = SUBSTEPS // snaps
    count = count_ref[0]
    sea = sea_ref[...].astype(F32)
    row = lax.broadcasted_iota(jnp.int32, (rows, cols), 0)
    col = lax.broadcasted_iota(jnp.int32, (rows, cols), 1)
    first_row, last_row = row == 0, row == rows - 1
    first_col, last_col = col == 0, col == cols - 1
    zero = jnp.zeros((rows, cols), F32)
    disp = [[zero, zero], [zero, zero]]
    for step in range(SUBSTEPS):
        if step % per_snap == 0:
            now = step // per_snap
            weights = []
            for back in (False, True):
                snap = now if back else snaps - 1 - now
                sign = 1.0 if back else -1.0
                u = vel_ref[0, snap, 0].astype(F32) * sea * sign
                v = vel_ref[0, snap, 1].astype(F32) * sea * sign
                up = jnp.where(first_row, 0.0, jnp.maximum(u, 0.0))
                un = jnp.where(last_row, 0.0, jnp.minimum(u, 0.0))
                vp = jnp.where(first_col, 0.0, jnp.maximum(v, 0.0))
                vn = jnp.where(last_col, 0.0, jnp.minimum(v, 0.0))
                own = 1.0 - (up - un) - (vp - vn)
                weights.append((own, up, un, vp, vn, u, v))
        for k in range(2):
            own, up, un, vp, vn, u, v = weights[k]
            fresh = []
            for comp in range(2):
                d = disp[k][comp]
                new = (
                    own * d
                    + up * pltpu.roll(d, 1, 0)
                    - un * pltpu.roll(d, rows - 1, 0)
                    + vp * pltpu.roll(d, 1, 1)
                    - vn * pltpu.roll(d, cols - 1, 1)
                    - (u, v)[comp]
                )
                fresh.append(jnp.where(step < count, new, d))
            disp[k] = fresh
    for k in range(2):
        for comp in range(2):
            out_ref[2 * k + comp] = disp[k][comp]


def join(first, then):
    e0, e1, e2, e3, e4, e5 = first
    l0, l1, l2, l3, l4, l5 = then
    return [
        l0 * e0 + l1 * e2,
        l0 * e1 + l1 * e3,
        l2 * e0 + l3 * e2,
        l2 * e1 + l3 * e3,
        l4 + l0 * e4 + l1 * e5,
        l5 + l2 * e4 + l3 * e5,
    ]


def strain(s):
    a11, a12, a21, a22, _, _ = s
    return [a11 * a11 + a21 * a21, a11 * a12 + a21 * a22, a12 * a12 + a22 * a22]


def hats(offset):
    hat = jnp.maximum(RADIUS + 1 - jnp.abs(offset), 0)
    return hat.astype(BF16), (hat * offset).astype(BF16)


def split(x):
    high = x.astype(BF16)
    return high, (x - high.astype(F32)).astype(BF16)


def dot(a, b):
    return jnp.dot(a, b, preferred_element_type=F32)


def slab_kernel(bits, me_ref, *refs):
    disp_refs, (send_ref, inner_ref, data) = refs[:4], refs[4:]
    me = me_ref[0]
    core = me % 2
    spot = me % 4
    comps, rows, cols = disp_refs[0].shape
    half = cols // 2
    block = comps * rows
    near = pl.multiple_of(core * half, LANES)
    far = pl.multiple_of(half - core * LANES, LANES)
    for k in range(4):
        place = pl.multiple_of((spot ^ k) * block, block)
        data[pl.ds(place, block), :half] = disp_refs[k][:, :, pl.ds(near, half)].reshape(block, half)
        data[pl.ds(place, block), half:] = disp_refs[k][:, :, pl.ds(far, LANES)].reshape(block, LANES)
    wide = half + LANES
    source = lax.broadcasted_iota(jnp.int32, (wide, half), 0)
    source = jnp.where(source < half, source + near, source - half + far)
    target = lax.broadcasted_iota(jnp.int32, (wide, half), 1) + near
    smooth_cols, slope_cols = hats(source - target)
    tall = 4 * block
    above = lax.broadcasted_iota(jnp.int32, (tall, tall), 0)
    below = lax.broadcasted_iota(jnp.int32, (tall, tall), 1)
    offset = jnp.where(above // rows == below // rows, below - above, RADIUS + 1)
    smooth_rows, slope_rows = hats(offset)
    high, low = split(data[...])
    along = dot(high, smooth_cols) + dot(low, smooth_cols)
    across = dot(high, slope_cols) + dot(low, slope_cols)
    high, low = split(along)
    grad_x = dot(slope_rows, high) + dot(slope_rows, low)
    high, low = split(across)
    grad_y = dot(smooth_rows, high) + dot(smooth_rows, low)
    total = sum(RADIUS + 1 - abs(o) for o in range(-RADIUS, RADIUS + 1))
    moment = sum((RADIUS + 1 - abs(o)) * o * o for o in range(-RADIUS, RADIUS + 1))
    scale = 1.0 / (total * moment)
    grad_x = grad_x * scale
    grad_y = grad_y * scale

    def state(window, direction):
        one = (window * comps + 2 * direction) * rows
        two = one + rows
        return [
            1.0 + grad_x[one : one + rows],
            grad_y[one : one + rows],
            grad_x[two : two + rows],
            1.0 + grad_y[two : two + rows],
            data[one : one + rows, :half],
            data[two : two + rows, :half],
        ]

    upper = spot >= 2
    products = []
    for direction in range(2):
        order = (0, 1, 2, 3) if direction == 0 else (3, 2, 1, 0)
        run = [state(order[0], direction)]
        for window in order[1:]:
            run.append(join(run[-1], state(window, direction)))
        products.append(run)
    fwd, bwd = products
    for k in range(6):
        for c in range(2):
            inner_ref[c, 0, k] = jnp.where(upper, fwd[2 + c][k], fwd[c][k])
            inner_ref[c, 1, k] = jnp.where(upper, bwd[1 - c][k], bwd[3 - c][k])
        for b in range(bits):
            low_side = (me // 4) & (1 << b) == 0
            send_ref[b, k] = jnp.where(low_side, fwd[3][k], bwd[3][k])


def finish_kernel(slabs, me_ref, inner_ref, *refs):
    others, (mine_ref, theirs_ref, totals) = refs[: slabs - 1], refs[slabs - 1 :]
    me = me_ref[0]
    core = me % 2
    slab = me // 4
    shape = inner_ref.shape[3:]
    for d in range(1, slabs):
        totals[slab ^ d] = others[d - 1][...]

    def load(k):
        return [totals[k, c] for c in range(6)]

    zero, one = jnp.zeros(shape, F32), jnp.ones(shape, F32)
    ident = [one, zero, zero, one, zero, zero]
    before = lax.fori_loop(0, slab, lambda k, run: join(run, load(k)), ident)
    after = lax.fori_loop(0, slabs - 1 - slab, lambda k, run: join(run, load(slabs - 1 - k)), ident)
    for flip, ref in ((0, mine_ref), (1, theirs_ref)):
        window = core ^ flip
        fwd = join(before, [inner_ref[window, 0, c] for c in range(6)])
        bwd = join(after, [inner_ref[window, 1, c] for c in range(6)])
        for k, plane in enumerate(strain(fwd) + strain(bwd) + fwd[4:] + bwd[4:]):
            ref[k] = plane


def place_kernel(me_ref, mine_ref, theirs_ref, *out_refs):
    core = me_ref[0] % 2
    half = mine_ref.shape[-1]
    near = pl.multiple_of(core * half, LANES)
    far = pl.multiple_of(half - core * half, LANES)
    start = 0
    for ref in out_refs:
        planes = ref.shape[1]
        ref[0, :, :, pl.ds(near, half)] = mine_ref[start : start + planes]
        ref[0, :, :, pl.ds(far, half)] = theirs_ref[start : start + planes]
        start += planes


SMEM = pl.BlockSpec(memory_space=pltpu.SMEM)
VMEM = pl.BlockSpec(memory_space=pltpu.VMEM)


def shards(velocity, substep_count, sea_mask, *, windows):
    rows, cols = sea_mask.shape
    half = cols // 2
    slabs = windows // 4
    bits = max(slabs - 1, 1).bit_length()
    me = lax.axis_index("tm").astype(jnp.int32)[None]

    def swap(x, d):
        return lax.ppermute(x, "tm", [(i, i ^ d) for i in range(windows)])

    def sds(*shape):
        return jax.ShapeDtypeStruct(shape, F32)

    disp = pl.pallas_call(
        advance_kernel, out_shape=sds(4, rows, cols), in_specs=[SMEM, VMEM, VMEM], out_specs=VMEM
    )(substep_count, velocity, sea_mask)
    next_core = swap(disp, 1)
    next_chip = swap(disp, 2)
    diagonal = swap(next_chip, 1)
    sends, inner = pl.pallas_call(
        functools.partial(slab_kernel, bits),
        out_shape=(sds(bits, 6, rows, half), sds(2, 2, 6, rows, half)),
        in_specs=[SMEM] + [VMEM] * 4,
        out_specs=(VMEM, VMEM),
        scratch_shapes=[pltpu.VMEM((16 * rows, half + LANES), F32)],
    )(me, disp, next_core, next_chip, diagonal)
    others = [swap(sends[d.bit_length() - 1], 4 * d) for d in range(1, slabs)]
    mine, theirs = pl.pallas_call(
        functools.partial(finish_kernel, slabs),
        out_shape=(sds(10, rows, half), sds(10, rows, half)),
        in_specs=[SMEM] + [VMEM] * slabs,
        out_specs=(VMEM, VMEM),
        scratch_shapes=[pltpu.VMEM((slabs, 6, rows, half), F32)],
    )(me, inner, *others)
    theirs = swap(theirs, 1)
    return pl.pallas_call(
        place_kernel,
        out_shape=(sds(1, 3, rows, cols), sds(1, 3, rows, cols), sds(1, 2, rows, cols), sds(1, 2, rows, cols)),
        in_specs=[SMEM, VMEM, VMEM],
        out_specs=(VMEM,) * 4,
    )(me, mine, theirs)


def solution(mesh):
    return jax.shard_map(
        functools.partial(shards, windows=mesh.shape["tm"]),
        mesh=mesh,
        in_specs=(P("tm", None, None, "groups", None), P("tm"), P("groups", None)),
        out_specs=(P("tm", None, "groups", None),) * 4,
        check_vma=False,
    )
```

```python
import functools

import jax
import jax.numpy as jnp
from jax import lax
from jax.experimental import pallas as pl
from jax.experimental.pallas import tpu as pltpu
from jax.sharding import PartitionSpec as P

SUBSTEPS = 12
RADIUS = 4
LANES = 128
TILE = 8
F32 = jnp.float32
BF16 = jnp.bfloat16


def join(first, then):
    e0, e1, e2, e3, e4, e5 = first
    l0, l1, l2, l3, l4, l5 = then
    return [
        l0 * e0 + l1 * e2,
        l0 * e1 + l1 * e3,
        l2 * e0 + l3 * e2,
        l2 * e1 + l3 * e3,
        l4 + l0 * e4 + l1 * e5,
        l5 + l2 * e4 + l3 * e5,
    ]


def pick(flag, yes, no):
    return [jnp.where(flag, a, b) for a, b in zip(yes, no)]


def join_ordered(flag, a, b):
    return join(pick(flag, a, b), pick(flag, b, a))


def strain(s):
    a11, a12, a21, a22, _, _ = s
    return [a11 * a11 + a21 * a21, a11 * a12 + a21 * a22, a12 * a12 + a22 * a22]


def planes(ref, *at):
    return [ref[(*at, k)] for k in range(6)]


def put(ref, values, *at):
    for k, value in enumerate(values):
        ref[(*at, k)] = value


def identity(shape):
    zero, one = jnp.zeros(shape, F32), jnp.ones(shape, F32)
    return [one, zero, zero, one, zero, zero]


def advance_kernel(me_ref, count_hbm, vel_hbm, sea_hbm, near_ref, far_ref, count_ref, vel_ref, sea_ref, sems):
    copies = [
        pltpu.make_async_copy(count_hbm, count_ref, sems.at[0]),
        pltpu.make_async_copy(vel_hbm, vel_ref, sems.at[1]),
        pltpu.make_async_copy(sea_hbm, sea_ref, sems.at[2]),
    ]
    for copy in copies:
        copy.start()
    for copy in copies:
        copy.wait()
    snaps, _, rows, cols = vel_ref.shape[1:]
    per_snap = SUBSTEPS // snaps
    count = count_ref[0, 0]
    sea = sea_ref[...].astype(F32)
    row = lax.broadcasted_iota(jnp.int32, (rows, cols), 0)
    col = lax.broadcasted_iota(jnp.int32, (rows, cols), 1)
    first_row, last_row = row == 0, row == rows - 1
    first_col, last_col = col == 0, col == cols - 1
    zero = jnp.zeros((rows, cols), F32)
    disp = [[zero, zero], [zero, zero]]
    for step in range(SUBSTEPS):
        if step % per_snap == 0:
            now = step // per_snap
            weights = []
            for back in (False, True):
                snap = now if back else snaps - 1 - now
                sign = 1.0 if back else -1.0
                u = vel_ref[0, snap, 0].astype(F32) * sea * sign
                v = vel_ref[0, snap, 1].astype(F32) * sea * sign
                up = jnp.where(first_row, 0.0, jnp.maximum(u, 0.0))
                un = jnp.where(last_row, 0.0, jnp.minimum(u, 0.0))
                vp = jnp.where(first_col, 0.0, jnp.maximum(v, 0.0))
                vn = jnp.where(last_col, 0.0, jnp.minimum(v, 0.0))
                own = 1.0 - (up - un) - (vp - vn)
                weights.append((own, up, un, vp, vn, u, v))
        for k in range(2):
            own, up, un, vp, vn, u, v = weights[k]
            fresh = []
            for comp in range(2):
                d = disp[k][comp]
                new = (
                    own * d
                    + up * pltpu.roll(d, 1, 0)
                    - un * pltpu.roll(d, rows - 1, 0)
                    + vp * pltpu.roll(d, 1, 1)
                    - vn * pltpu.roll(d, cols - 1, 1)
                    - (u, v)[comp]
                )
                fresh.append(jnp.where(step < count, new, d))
            disp[k] = fresh
    half = cols // 2
    lane = lax.broadcasted_iota(jnp.int32, (TILE, LANES), 1)
    core = me_ref[0] % 2
    parcels = []
    for side in range(2):
        body = [d[:, side * half : (side + 1) * half] for pair in disp for d in pair]
        at = half if side == 0 else half - LANES
        shift = 0 if side == 0 else RADIUS
        halo = jnp.zeros((TILE, LANES), F32)
        spot = 0
        for pair in disp:
            for d in pair:
                for r in range(0, rows, TILE):
                    edge = d[r : r + TILE, at : at + LANES]
                    turn = (spot + shift) % LANES
                    edge = pltpu.roll(edge, turn, 1) if turn else edge
                    halo = jnp.where((lane >= spot) & (lane < spot + RADIUS), edge, halo)
                    spot += RADIUS
        parcels.append((body, halo))

    def write(ref, parcel):
        body, halo = parcel
        for k, value in enumerate(body):
            ref[k * rows : (k + 1) * rows] = value
        end = len(body) * rows
        ref[end:, :LANES] = halo
        ref[end:, LANES:] = jnp.zeros((TILE, half - LANES), F32)

    @pl.when(core == 0)
    def _():
        write(near_ref, parcels[0])
        write(far_ref, parcels[1])

    @pl.when(core != 0)
    def _():
        write(near_ref, parcels[1])
        write(far_ref, parcels[0])


def hats(offset):
    hat = jnp.maximum(RADIUS + 1 - jnp.abs(offset), 0)
    return hat.astype(BF16), (hat * offset).astype(BF16)


def split(x):
    high = x.astype(BF16)
    return high, (x - high.astype(F32)).astype(BF16)


def dot(a, b):
    return jnp.dot(a, b, preferred_element_type=F32)


def make_tables(core, rows, half, cols_ref, rows_ref):
    wide = half + LANES
    source = lax.broadcasted_iota(jnp.int32, (wide, half), 0)
    target = lax.broadcasted_iota(jnp.int32, (wide, half), 1)
    beside = source - half
    halo = jnp.where(core == 0, source, beside - RADIUS)
    offset = jnp.where(source < half, source, halo) - target
    offset = jnp.where(beside < RADIUS, offset, RADIUS + 1)
    smooth, slope = hats(offset)
    cols_ref[:, :half] = smooth
    cols_ref[:, half:] = slope
    tall = 4 * rows
    above = lax.broadcasted_iota(jnp.int32, (tall, tall), 0)
    below = lax.broadcasted_iota(jnp.int32, (tall, tall), 1)
    offset = jnp.where(above // rows == below // rows, below - above, RADIUS + 1)
    smooth, slope = hats(offset)
    rows_ref[0] = smooth
    rows_ref[1] = slope


def states(parcel_refs, table, rows_ref):
    half = parcel_refs[0].shape[1]
    tall = parcel_refs[0].shape[0] - TILE
    rows = tall // 4
    bodies, wide = [], []
    for ref in parcel_refs:
        packed = ref[tall:, :LANES]
        halo = [packed]
        for k in range(1, tall // TILE):
            halo.append(pltpu.roll(packed, LANES - k * RADIUS, 1))
        bodies.append(ref[:tall])
        wide.append(jnp.concatenate([bodies[-1], jnp.concatenate(halo, axis=0)], axis=1))
    high, low = split(jnp.concatenate(wide, axis=0))
    along = dot(high, table) + dot(low, table)
    smooth, slope = rows_ref[0], rows_ref[1]
    total = sum(RADIUS + 1 - abs(o) for o in range(-RADIUS, RADIUS + 1))
    moment = sum((RADIUS + 1 - abs(o)) * o * o for o in range(-RADIUS, RADIUS + 1))
    scale = 1.0 / (total * moment)
    result = []
    for k, body in enumerate(bodies):
        high, low = split(along[k * tall : (k + 1) * tall])
        grad_x = (dot(slope, high[:, :half]) + dot(slope, low[:, :half])) * scale
        grad_y = (dot(smooth, high[:, half:]) + dot(smooth, low[:, half:])) * scale
        maps = []
        for direction in range(2):
            one = slice(2 * direction * rows, (2 * direction + 1) * rows)
            two = slice((2 * direction + 1) * rows, (2 * direction + 2) * rows)
            maps.append([1.0 + grad_x[one], grad_y[one], grad_x[two], 1.0 + grad_y[two], body[one], body[two]])
        result.append(maps)
    return result


def chip_kernel(me_ref, own_ref, next_ref, inner_ref, cols_ref, rows_ref):
    core = me_ref[0] % 2
    rows, half = inner_ref.shape[3:]
    make_tables(core, rows, half, cols_ref, rows_ref)
    own, other = states((own_ref, next_ref), cols_ref[...], rows_ref)
    first = core == 0
    a, b = pick(first, own[0], other[0]), pick(first, other[0], own[0])
    put(inner_ref, a, 0, 0)
    put(inner_ref, join(a, b), 1, 0)
    a, b = pick(first, own[1], other[1]), pick(first, other[1], own[1])
    put(inner_ref, b, 1, 1)
    put(inner_ref, join(b, a), 0, 1)


def slab_kernel(me_ref, inner_ref, straight_ref, across_ref, cols_ref, rows_ref, urgent_ref, other_ref, outer_ref):
    me = me_ref[0]
    first = me % 2 == 0
    lower = me // 2 % 2 == 0
    straight, across = states((straight_ref, across_ref), cols_ref[...], rows_ref)
    beside_fwd = join_ordered(first, straight[0], across[0])
    beside_bwd = join_ordered(first, across[1], straight[1])
    total_fwd = join_ordered(lower, planes(inner_ref, 1, 0), beside_fwd)
    total_bwd = join_ordered(lower, beside_bwd, planes(inner_ref, 0, 1))
    ident = identity(total_fwd[0].shape)
    put(outer_ref, pick(lower, ident, beside_fwd), 0)
    put(outer_ref, pick(lower, beside_bwd, ident), 1)
    forward = me // 8 % 2 == 0
    put(urgent_ref, pick(forward, total_fwd, total_bwd))
    put(other_ref, pick(forward, total_bwd, total_fwd))


def level_kernel(level, me_ref, urgent_ref, other_ref, outer_ref, got_urgent_ref, got_other_ref, *out_refs):
    next_urgent_ref, next_other_ref, next_outer_ref = out_refs
    slab = me_ref[0] // 4
    lower = slab // 2**level % 2 == 0
    forward = slab // 2 ** (level + 1) % 2 == 0
    urgent, other = planes(urgent_ref), planes(other_ref)
    got_urgent, got_other = planes(got_urgent_ref), planes(got_other_ref)
    fwd, bwd = pick(forward, urgent, other), pick(forward, other, urgent)
    got_fwd, got_bwd = pick(forward, got_urgent, got_other), pick(forward, got_other, got_urgent)
    outer_fwd, outer_bwd = planes(outer_ref, 0), planes(outer_ref, 1)
    put(next_outer_ref, pick(lower, outer_fwd, join(got_fwd, outer_fwd)), 0)
    put(next_outer_ref, pick(lower, join(got_bwd, outer_bwd), outer_bwd), 1)
    fwd, bwd = join_ordered(lower, fwd, got_fwd), join_ordered(lower, got_bwd, bwd)
    forward = slab // 2 ** (level + 2) % 2 == 0
    put(next_urgent_ref, pick(forward, fwd, bwd))
    put(next_other_ref, pick(forward, bwd, fwd))


def urgent_kernel(level, me_ref, urgent_ref, got_ref, out_ref):
    slab = me_ref[0] // 4
    lower = slab // 2**level % 2 == 0
    forward = slab // 2 ** (level + 1) % 2 == 0
    put(out_ref, join_ordered(lower == forward, planes(urgent_ref), planes(got_ref)))


def finish_kernel(level, me_ref, inner_ref, outer_ref, urgent_ref, other_ref, last_ref, mine_ref, theirs_ref):
    me = me_ref[0]
    core = me % 2
    slab = me // 4
    lower = slab // 2**level % 2 == 0
    forward = slab // 2 ** (level + 1) % 2 == 0
    near = pick(lower == forward, planes(other_ref), planes(urgent_ref))
    last = planes(last_ref)
    before, after = planes(outer_ref, 0), planes(outer_ref, 1)
    before = pick(lower, before, join(near, before))
    after = pick(lower, join(near, after), after)
    before = pick(forward, before, join(last, before))
    after = pick(forward, join(last, after), after)
    for flip, ref in ((0, mine_ref), (1, theirs_ref)):
        window = core ^ flip
        fwd = join(before, planes(inner_ref, window, 0))
        bwd = join(after, planes(inner_ref, window, 1))
        for k, plane in enumerate(strain(fwd) + strain(bwd) + fwd[4:] + bwd[4:]):
            ref[k] = plane


def place_kernel(me_ref, mine_ref, theirs_ref, *refs):
    out_refs, sems = refs[:-1], refs[-1]
    core = me_ref[0] % 2
    half = mine_ref.shape[-1]
    near = pl.multiple_of(core * half, LANES)
    far = pl.multiple_of(half - core * half, LANES)
    copies = []
    for source, at in ((mine_ref, near), (theirs_ref, far)):
        start = 0
        for ref in out_refs:
            many = ref.shape[1]
            target = ref.at[0, :, :, pl.ds(at, half)]
            copies.append(pltpu.make_async_copy(source.at[start : start + many], target, sems.at[len(copies)]))
            start += many
    for copy in copies:
        copy.start()
    for copy in copies:
        copy.wait()


SMEM = pl.BlockSpec(memory_space=pltpu.SMEM)
VMEM = pl.BlockSpec(memory_space=pltpu.VMEM)
HBM = pl.BlockSpec(memory_space=pltpu.HBM)
PARAMS = pltpu.CompilerParams(vmem_limit_bytes=8 * 1024 * 1024)


def sds(*shape, dtype=F32):
    return jax.ShapeDtypeStruct(shape, dtype)


def call(kernel, outs, *args, specs=None, out_specs=None, scratch=()):
    specs = specs or [SMEM] * (args[0].ndim == 1) + [VMEM] * (len(args) - (args[0].ndim == 1))
    many = isinstance(outs, tuple)
    out_specs = out_specs or ((VMEM,) * len(outs) if many else VMEM)
    return pl.pallas_call(
        kernel,
        out_shape=outs,
        in_specs=specs,
        out_specs=out_specs,
        scratch_shapes=scratch,
        compiler_params=PARAMS,
    )(*args)


def shards(velocity, substep_count, sea_mask, *, windows):
    rows, cols = sea_mask.shape
    half = cols // 2
    slabs = windows // 4
    last_level = slabs.bit_length() - 2
    me = lax.axis_index("tm").astype(jnp.int32)[None]

    def swap(x, d, keep=lambda i: True):
        return lax.ppermute(x, "tm", [(i, i ^ d) for i in range(windows) if keep(i)])

    tall = 4 * rows + TILE
    near, far = call(
        advance_kernel,
        (sds(tall, half), sds(tall, half)),
        me,
        substep_count[None], *(pltpu.with_memory_space_constraint(x, pltpu.HBM) for x in (velocity, sea_mask)),
        specs=[SMEM, HBM, HBM, HBM],
        scratch=[
            pltpu.SMEM((1, 1), jnp.int32),
            pltpu.VMEM(velocity.shape, velocity.dtype),
            pltpu.VMEM(sea_mask.shape, sea_mask.dtype),
            pltpu.SemaphoreType.DMA((3,)),
        ],
    )
    straight = swap(near, 2)
    across = swap(far, 3)
    next_core = swap(far, 1)
    one, both = sds(6, rows, half), sds(2, 6, rows, half)
    inner, col_table, row_table = call(
        chip_kernel,
        (
            sds(2, 2, 6, rows, half),
            sds(half + LANES, cols, dtype=BF16),
            sds(2, 4 * rows, 4 * rows, dtype=BF16),
        ),
        me,
        near,
        next_core,
    )
    urgent, other, outer = call(
        slab_kernel, (one, one, both), me, inner, straight, across, col_table, row_table
    )
    for level in range(last_level - 1):
        urgent, other, outer = call(
            functools.partial(level_kernel, level),
            (one, one, both),
            me,
            urgent,
            other,
            outer,
            swap(urgent, 4 << level),
            swap(other, 4 << level),
        )
    level = last_level - 1

    def sends_other(i):
        return (i // 4 >> level) % 2 != (i // 4 >> last_level) % 2

    got_urgent = swap(urgent, 4 << level)
    got_other = swap(other, 4 << level, sends_other)
    urgent = call(functools.partial(urgent_kernel, level), one, me, urgent, got_urgent)
    last = swap(urgent, 4 << last_level)
    ten = sds(10, rows, half)
    mine, theirs = call(
        functools.partial(finish_kernel, level), (ten, ten), me, inner, outer, got_urgent, got_other, last
    )
    theirs = swap(theirs, 1)
    return call(
        place_kernel,
        (sds(1, 3, rows, cols), sds(1, 3, rows, cols), sds(1, 2, rows, cols), sds(1, 2, rows, cols)),
        me,
        mine,
        theirs,
        out_specs=(HBM,) * 4,
        scratch=[pltpu.SemaphoreType.DMA((8,))],
    )


def solution(mesh):
    return jax.shard_map(
        functools.partial(shards, windows=mesh.shape["tm"]),
        mesh=mesh,
        in_specs=(P("tm", None, None, "groups", None), P("tm"), P("groups", None)),
        out_specs=(P("tm", None, "groups", None),) * 4,
        check_vma=False,
    )
```

```python
import functools

import jax
import jax.numpy as jnp
from jax import lax
from jax.experimental import pallas as pl
from jax.experimental.pallas import tpu as pltpu
from jax.sharding import PartitionSpec as P

SUBSTEPS = 12
RADIUS = 4
LANES = 128
TILE = 8
F32 = jnp.float32
BF16 = jnp.bfloat16


def join(first, then):
    e0, e1, e2, e3, e4, e5 = first
    l0, l1, l2, l3, l4, l5 = then
    return [
        l0 * e0 + l1 * e2,
        l0 * e1 + l1 * e3,
        l2 * e0 + l3 * e2,
        l2 * e1 + l3 * e3,
        l4 + l0 * e4 + l1 * e5,
        l5 + l2 * e4 + l3 * e5,
    ]


def pick(flag, yes, no):
    return [jnp.where(flag, a, b) for a, b in zip(yes, no)]


def join_ordered(flag, a, b):
    return join(pick(flag, a, b), pick(flag, b, a))


def strain(s):
    a11, a12, a21, a22, _, _ = s
    return [a11 * a11 + a21 * a21, a11 * a12 + a21 * a22, a12 * a12 + a22 * a22]


def planes(ref, *at):
    return [ref[(*at, k)] for k in range(6)]


def put(ref, values, *at):
    for k, value in enumerate(values):
        ref[(*at, k)] = value


def identity(shape):
    zero, one = jnp.zeros(shape, F32), jnp.ones(shape, F32)
    return [one, zero, zero, one, zero, zero]


def advance_kernel(me_ref, count_hbm, vel_hbm, sea_hbm, near_ref, far_ref, count_ref, vel_ref, sea_ref, flow_ref, sems):
    snaps, _, rows, cols = vel_ref.shape[1:]
    wait_for = [
        pltpu.make_async_copy(vel_hbm.at[0, snap], vel_ref.at[0, snap], sems.at[2 + snap]) for snap in range(snaps)
    ]
    load_sea = pltpu.make_async_copy(sea_hbm, sea_ref, sems.at[0])
    load_count = pltpu.make_async_copy(count_hbm, count_ref, sems.at[1])
    load_sea.start()
    for now in range(snaps // 2):
        wait_for[now].start()
        wait_for[snaps - 1 - now].start()
    load_count.start()
    load_sea.wait()
    load_count.wait()
    per_snap = SUBSTEPS // snaps
    count = count_ref[0, 0]
    sea = sea_ref[...].astype(F32)

    def flow_in(snap):
        wait_for[snap].wait()
        for comp in range(2):
            flow = vel_ref[0, snap, comp].astype(F32) * sea
            for piece in range(cols // LANES):
                flow_ref[snap, comp, piece] = flow[:, piece * LANES : (piece + 1) * LANES]

    deep = rows // 2

    def flow_of(snap, comp, odd):
        pieces = [flow_ref[snap, comp, piece, pl.ds(odd, deep, stride=2), :] for piece in range(cols // LANES)]
        return jnp.concatenate(pieces, axis=1)

    row = lax.broadcasted_iota(jnp.int32, (deep, cols), 0)
    col = lax.broadcasted_iota(jnp.int32, (deep, cols), 1)
    first_col, last_col = col == 0, col == cols - 1
    zero = jnp.zeros((deep, cols), F32)
    disp = [[[zero, zero], [zero, zero]], [[zero, zero], [zero, zero]]]
    for step in range(SUBSTEPS):
        if step % per_snap == 0:
            now = step // per_snap
            if now < snaps // 2:
                flow_in(now)
                flow_in(snaps - 1 - now)
            weights = []
            for back in (False, True):
                snap = now if back else snaps - 1 - now
                sign = 1.0 if back else -1.0
                pair = []
                for odd in range(2):
                    u = flow_of(snap, 0, odd) * sign
                    v = flow_of(snap, 1, odd) * sign
                    up, un = jnp.maximum(u, 0.0), jnp.minimum(u, 0.0)
                    if odd:
                        un = jnp.where(row == deep - 1, 0.0, un)
                    else:
                        up = jnp.where(row == 0, 0.0, up)
                    vp = jnp.where(first_col, 0.0, jnp.maximum(v, 0.0))
                    vn = jnp.where(last_col, 0.0, jnp.minimum(v, 0.0))
                    own = 1.0 - (up - un) - (vp - vn)
                    pair.append((own, up, un, vp, vn, u, v))
                weights.append(pair)
        for k in range(2):
            for comp in range(2):
                even, odd = disp[k][comp]
                above = (pltpu.roll(odd, 1, 0), even)
                below = (odd, pltpu.roll(even, deep - 1, 0))
                fresh = []
                for parity, d in enumerate((even, odd)):
                    own, up, un, vp, vn, u, v = weights[k][parity]
                    new = (
                        own * d
                        + up * above[parity]
                        - un * below[parity]
                        + vp * pltpu.roll(d, 1, 1)
                        - vn * pltpu.roll(d, cols - 1, 1)
                        - (u, v)[comp]
                    )
                    fresh.append(jnp.where(step < count, new, d))
                disp[k][comp] = fresh
    half = cols // 2
    tiles = [d for pair in disp for plane in pair for d in plane]
    lane = lax.broadcasted_iota(jnp.int32, (deep, LANES), 1)
    core = me_ref[0] % 2
    for side in range(2):
        at = half if side == 0 else half - LANES
        shift = 0 if side == 0 else RADIUS
        halo = jnp.zeros((deep, LANES), F32)
        for k, d in enumerate(tiles):
            turn = (k * RADIUS + shift) % LANES
            edge = d[:, at : at + LANES]
            edge = pltpu.roll(edge, turn, 1) if turn else edge
            halo = jnp.where((lane >= k * RADIUS) & (lane < (k + 1) * RADIUS), edge, halo)

        def write(ref):
            for piece in range(half // LANES):
                start = side * half + piece * LANES
                for k, d in enumerate(tiles):
                    place = (piece * len(tiles) + k) * deep
                    ref[place : place + deep] = d[:, start : start + LANES]
            ref[half // LANES * len(tiles) * deep :] = halo

        @pl.when(core == side)
        def _():
            write(near_ref)

        @pl.when(core != side)
        def _():
            write(far_ref)


def hats(offset):
    hat = jnp.maximum(RADIUS + 1 - jnp.abs(offset), 0)
    return hat.astype(BF16), (hat * offset).astype(BF16)


def split(x):
    high = x.astype(BF16)
    return high, (x - high.astype(F32)).astype(BF16)


def dot(a, b):
    return jnp.dot(a, b, preferred_element_type=F32)


def make_tables(core, rows, half, cols_ref, rows_ref):
    wide = half + LANES
    source = lax.broadcasted_iota(jnp.int32, (wide, half), 0)
    target = lax.broadcasted_iota(jnp.int32, (wide, half), 1)
    beside = source - half
    halo = jnp.where(core == 0, source, beside - RADIUS)
    offset = jnp.where(source < half, source, halo) - target
    offset = jnp.where(beside < RADIUS, offset, RADIUS + 1)
    smooth, slope = hats(offset)
    cols_ref[:, :half] = smooth
    cols_ref[:, half:] = slope
    tall = 4 * rows
    above = lax.broadcasted_iota(jnp.int32, (tall, tall), 0)
    below = lax.broadcasted_iota(jnp.int32, (tall, tall), 1)
    deep = rows // 2

    def natural(place):
        return place % deep * 2 + place % rows // deep

    offset = jnp.where(above // rows == below // rows, natural(below) - natural(above), RADIUS + 1)
    smooth, slope = hats(offset)
    for part in range(2):
        rows_ref[0, :, part * tall : (part + 1) * tall] = smooth
        rows_ref[1, :, part * tall : (part + 1) * tall] = slope


def states(parcel_refs, table, rows_ref):
    half = table.shape[1] // 2
    tall = rows_ref.shape[1]
    rows = tall // 4
    bodies, wide = [], []
    for ref in parcel_refs:
        body = [ref[k * tall : (k + 1) * tall] for k in range(half // LANES)]
        packed = ref[half // LANES * tall :]
        halo = [packed]
        for k in range(1, tall // TILE):
            halo.append(pltpu.roll(packed, LANES - k * RADIUS, 1))
        bodies.append(jnp.concatenate(body, axis=1))
        wide.append(jnp.concatenate([*body, jnp.concatenate(halo, axis=0)], axis=1))
    many = len(wide) * tall
    along = dot(jnp.concatenate(split(jnp.concatenate(wide, axis=0)), axis=0), table)
    along = along[:many] + along[many:]
    smooth, slope = rows_ref[0], rows_ref[1]
    total = sum(RADIUS + 1 - abs(o) for o in range(-RADIUS, RADIUS + 1))
    moment = sum((RADIUS + 1 - abs(o)) * o * o for o in range(-RADIUS, RADIUS + 1))
    scale = 1.0 / (total * moment)
    result = []
    for k, body in enumerate(bodies):
        parts = jnp.concatenate(split(along[k * tall : (k + 1) * tall]), axis=0)
        grad_x = dot(slope, parts[:, :half]) * scale
        grad_y = dot(smooth, parts[:, half:]) * scale
        maps = []
        for direction in range(2):
            one = slice(2 * direction * rows, (2 * direction + 1) * rows)
            two = slice((2 * direction + 1) * rows, (2 * direction + 2) * rows)
            maps.append([1.0 + grad_x[one], grad_y[one], grad_x[two], 1.0 + grad_y[two], body[one], body[two]])
        result.append(maps)
    return result


def chip_kernel(me_ref, own_ref, next_ref, inner_ref, cols_ref, rows_ref):
    core = me_ref[0] % 2
    rows, half = inner_ref.shape[3:]
    make_tables(core, rows, half, cols_ref, rows_ref)
    own, other = states((own_ref, next_ref), cols_ref[...], rows_ref)
    first = core == 0
    a, b = pick(first, own[0], other[0]), pick(first, other[0], own[0])
    put(inner_ref, a, 0, 0)
    put(inner_ref, join(a, b), 1, 0)
    a, b = pick(first, own[1], other[1]), pick(first, other[1], own[1])
    put(inner_ref, b, 1, 1)
    put(inner_ref, join(b, a), 0, 1)


def next_kernel(parcel_ref, cols_ref, rows_ref, state_ref):
    for direction, state in enumerate(states((parcel_ref,), cols_ref[...], rows_ref)[0]):
        put(state_ref, state, direction)


def slab_kernel(me_ref, inner_ref, straight_ref, across_ref, cols_ref, rows_ref, urgent_ref, other_ref, outer_ref):
    me = me_ref[0]
    first = me % 2 == 0
    lower = me // 2 % 2 == 0
    straight = planes(straight_ref, 0), planes(straight_ref, 1)
    across = states((across_ref,), cols_ref[...], rows_ref)[0]
    beside_fwd = join_ordered(first, straight[0], across[0])
    beside_bwd = join_ordered(first, across[1], straight[1])
    total_fwd = join_ordered(lower, planes(inner_ref, 1, 0), beside_fwd)
    total_bwd = join_ordered(lower, beside_bwd, planes(inner_ref, 0, 1))
    ident = identity(total_fwd[0].shape)
    put(outer_ref, pick(lower, ident, beside_fwd), 0)
    put(outer_ref, pick(lower, beside_bwd, ident), 1)
    forward = me // 8 % 2 == 0
    put(urgent_ref, pick(forward, total_fwd, total_bwd))
    put(other_ref, pick(forward, total_bwd, total_fwd))


def level_kernel(level, me_ref, urgent_ref, other_ref, outer_ref, got_urgent_ref, got_other_ref, *out_refs):
    next_urgent_ref, next_other_ref, next_outer_ref = out_refs
    slab = me_ref[0] // 4
    lower = slab // 2**level % 2 == 0
    forward = slab // 2 ** (level + 1) % 2 == 0
    urgent, other = planes(urgent_ref), planes(other_ref)
    got_urgent, got_other = planes(got_urgent_ref), planes(got_other_ref)
    fwd, bwd = pick(forward, urgent, other), pick(forward, other, urgent)
    got_fwd, got_bwd = pick(forward, got_urgent, got_other), pick(forward, got_other, got_urgent)
    outer_fwd, outer_bwd = planes(outer_ref, 0), planes(outer_ref, 1)
    put(next_outer_ref, pick(lower, outer_fwd, join(got_fwd, outer_fwd)), 0)
    put(next_outer_ref, pick(lower, join(got_bwd, outer_bwd), outer_bwd), 1)
    fwd, bwd = join_ordered(lower, fwd, got_fwd), join_ordered(lower, got_bwd, bwd)
    forward = slab // 2 ** (level + 2) % 2 == 0
    put(next_urgent_ref, pick(forward, fwd, bwd))
    put(next_other_ref, pick(forward, bwd, fwd))


def urgent_kernel(level, me_ref, urgent_ref, got_ref, out_ref):
    slab = me_ref[0] // 4
    lower = slab // 2**level % 2 == 0
    forward = slab // 2 ** (level + 1) % 2 == 0
    put(out_ref, join_ordered(lower == forward, planes(urgent_ref), planes(got_ref)))


def finish_kernel(level, me_ref, inner_ref, outer_ref, urgent_ref, other_ref, last_ref, mine_ref, theirs_ref):
    me = me_ref[0]
    core = me % 2
    slab = me // 4
    lower = slab // 2**level % 2 == 0
    forward = slab // 2 ** (level + 1) % 2 == 0
    near = pick(lower == forward, planes(other_ref), planes(urgent_ref))
    last = planes(last_ref)
    before, after = planes(outer_ref, 0), planes(outer_ref, 1)
    before = pick(lower, before, join(near, before))
    after = pick(lower, join(near, after), after)
    before = pick(forward, before, join(last, before))
    after = pick(forward, join(last, after), after)
    for flip, ref in ((0, mine_ref), (1, theirs_ref)):
        window = core ^ flip
        fwd = join(before, planes(inner_ref, window, 0))
        bwd = join(after, planes(inner_ref, window, 1))
        deep = ref.shape[2] // 2
        for k, plane in enumerate(strain(fwd) + strain(bwd) + fwd[4:] + bwd[4:]):
            for piece in range(ref.shape[1]):
                lanes = slice(piece * LANES, (piece + 1) * LANES)
                ref[k, piece, pl.ds(0, deep, stride=2), :] = plane[:deep, lanes]
                ref[k, piece, pl.ds(1, deep, stride=2), :] = plane[deep:, lanes]


def place_kernel(me_ref, mine_ref, theirs_ref, *refs):
    out_refs, sems = refs[:-1], refs[-1]
    core = me_ref[0] % 2
    pieces = mine_ref.shape[1]
    copies = []
    for source, side in ((mine_ref, core), (theirs_ref, 1 - core)):
        for piece in range(pieces):
            at = pl.multiple_of((side * pieces + piece) * LANES, LANES)
            start = 0
            for ref in out_refs:
                many = ref.shape[1]
                target = ref.at[0, :, :, pl.ds(at, LANES)]
                copies.append(
                    pltpu.make_async_copy(source.at[start : start + many, piece], target, sems.at[len(copies)])
                )
                start += many
    for copy in copies:
        copy.start()
    for copy in copies:
        copy.wait()


SMEM = pl.BlockSpec(memory_space=pltpu.SMEM)
VMEM = pl.BlockSpec(memory_space=pltpu.VMEM)
HBM = pl.BlockSpec(memory_space=pltpu.HBM)
PARAMS = pltpu.CompilerParams(vmem_limit_bytes=8 * 1024 * 1024)


def sds(*shape, dtype=F32):
    return jax.ShapeDtypeStruct(shape, dtype)


def call(kernel, outs, *args, specs=None, out_specs=None, scratch=()):
    specs = specs or [SMEM] * (args[0].ndim == 1) + [VMEM] * (len(args) - (args[0].ndim == 1))
    many = isinstance(outs, tuple)
    out_specs = out_specs or ((VMEM,) * len(outs) if many else VMEM)
    return pl.pallas_call(
        kernel,
        out_shape=outs,
        in_specs=specs,
        out_specs=out_specs,
        scratch_shapes=scratch,
        compiler_params=PARAMS,
    )(*args)


def shards(velocity, substep_count, sea_mask, *, windows):
    rows, cols = sea_mask.shape
    half = cols // 2
    slabs = windows // 4
    last_level = slabs.bit_length() - 2
    me = lax.axis_index("tm").astype(jnp.int32)[None]

    def swap(x, d, keep=lambda i: True):
        return lax.ppermute(x, "tm", [(i, i ^ d) for i in range(windows) if keep(i)])

    tall = 4 * rows * (half // LANES) + TILE
    near, far = call(
        advance_kernel,
        (sds(tall, LANES), sds(tall, LANES)),
        me,
        substep_count[None], *(pltpu.with_memory_space_constraint(x, pltpu.HBM) for x in (velocity, sea_mask)),
        specs=[SMEM, HBM, HBM, HBM],
        scratch=[
            pltpu.SMEM((1, 1), jnp.int32),
            pltpu.VMEM(velocity.shape, velocity.dtype),
            pltpu.VMEM(sea_mask.shape, sea_mask.dtype),
            pltpu.VMEM((*velocity.shape[1:3], cols // LANES, rows, LANES), F32),
            pltpu.SemaphoreType.DMA((2 + velocity.shape[1],)),
        ],
    )
    straight = swap(near, 2)
    across = swap(far, 3)
    next_core = swap(far, 1)
    one, both = sds(6, rows, half), sds(2, 6, rows, half)
    inner, col_table, row_table = call(
        chip_kernel,
        (
            sds(2, 2, 6, rows, half),
            sds(half + LANES, cols, dtype=BF16),
            sds(2, 4 * rows, 8 * rows, dtype=BF16),
        ),
        me,
        near,
        next_core,
    )
    straight = call(next_kernel, both, straight, col_table, row_table)
    urgent, other, outer = call(
        slab_kernel, (one, one, both), me, inner, straight, across, col_table, row_table
    )
    for level in range(last_level - 1):
        urgent, other, outer = call(
            functools.partial(level_kernel, level),
            (one, one, both),
            me,
            urgent,
            other,
            outer,
            swap(urgent, 4 << level),
            swap(other, 4 << level),
        )
    level = last_level - 1

    def sends_other(i):
        return (i // 4 >> level) % 2 != (i // 4 >> last_level) % 2

    got_urgent = swap(urgent, 4 << level)
    got_other = swap(other, 4 << level)
    urgent = call(functools.partial(urgent_kernel, level), one, me, urgent, got_urgent)
    last = swap(urgent, 4 << last_level)
    ten = sds(10, half // LANES, rows, LANES)
    mine, theirs = call(
        functools.partial(finish_kernel, level), (ten, ten), me, inner, outer, got_urgent, got_other, last
    )
    theirs = swap(theirs, 1)
    return call(
        place_kernel,
        (sds(1, 3, rows, cols), sds(1, 3, rows, cols), sds(1, 2, rows, cols), sds(1, 2, rows, cols)),
        me,
        mine,
        theirs,
        out_specs=(HBM,) * 4,
        scratch=[pltpu.SemaphoreType.DMA((8 * (half // LANES),))],
    )


def solution(mesh):
    return jax.shard_map(
        functools.partial(shards, windows=mesh.shape["tm"]),
        mesh=mesh,
        in_specs=(P("tm", None, None, "groups", None), P("tm"), P("groups", None)),
        out_specs=(P("tm", None, "groups", None),) * 4,
        check_vma=False,
    )
```

```python
import functools

import jax
import jax.numpy as jnp
from jax import lax
from jax.experimental import pallas as pl
from jax.experimental.pallas import tpu as pltpu
from jax.sharding import PartitionSpec as P

SUBSTEPS = 12
RADIUS = 4
LANES = 128
TILE = 8
F32 = jnp.float32
BF16 = jnp.bfloat16


def join(first, then):
    e0, e1, e2, e3, e4, e5 = first
    l0, l1, l2, l3, l4, l5 = then
    return [
        l0 * e0 + l1 * e2,
        l0 * e1 + l1 * e3,
        l2 * e0 + l3 * e2,
        l2 * e1 + l3 * e3,
        l4 + l0 * e4 + l1 * e5,
        l5 + l2 * e4 + l3 * e5,
    ]


def pick(flag, yes, no):
    return [jnp.where(flag, a, b) for a, b in zip(yes, no)]


def join_ordered(flag, a, b):
    return join(pick(flag, a, b), pick(flag, b, a))


def strain(s):
    a11, a12, a21, a22, _, _ = s
    return [a11 * a11 + a21 * a21, a11 * a12 + a21 * a22, a12 * a12 + a22 * a22]


def planes(ref, *at):
    return [ref[(*at, k)] for k in range(6)]


def put(ref, values, *at):
    for k, value in enumerate(values):
        ref[(*at, k)] = value


def identity(shape):
    zero, one = jnp.zeros(shape, F32), jnp.ones(shape, F32)
    return [one, zero, zero, one, zero, zero]


def advance_kernel(me_ref, count_ref, vel_hbm, sea_hbm, near_ref, far_ref, vel_ref, sea_ref, flow_ref, sems):
    snaps, _, rows, cols = vel_ref.shape[1:]
    wait_for = [
        pltpu.make_async_copy(vel_hbm.at[0, snap], vel_ref.at[0, snap], sems.at[2 + snap]) for snap in range(snaps)
    ]
    load_sea = pltpu.make_async_copy(sea_hbm, sea_ref, sems.at[0])
    load_sea.start()
    for now in range(snaps // 2):
        wait_for[now].start()
        wait_for[snaps - 1 - now].start()
    load_sea.wait()
    per_snap = SUBSTEPS // snaps
    count = count_ref[0]
    sea = sea_ref[...].astype(F32)

    def flow_in(snap):
        wait_for[snap].wait()
        for comp in range(2):
            flow = vel_ref[0, snap, comp].astype(F32) * sea
            for piece in range(cols // LANES):
                flow_ref[snap, comp, piece] = flow[:, piece * LANES : (piece + 1) * LANES]

    deep = rows // 2

    def flow_of(snap, comp, odd):
        pieces = [flow_ref[snap, comp, piece, pl.ds(odd, deep, stride=2), :] for piece in range(cols // LANES)]
        return jnp.concatenate(pieces, axis=1)

    row = lax.broadcasted_iota(jnp.int32, (deep, cols), 0)
    col = lax.broadcasted_iota(jnp.int32, (deep, cols), 1)
    first_col, last_col = col == 0, col == cols - 1
    zero = jnp.zeros((deep, cols), F32)
    disp = [[[zero, zero], [zero, zero]], [[zero, zero], [zero, zero]]]
    for step in range(SUBSTEPS):
        if step % per_snap == 0:
            now = step // per_snap
            if now < snaps // 2:
                flow_in(now)
                flow_in(snaps - 1 - now)
            weights = []
            for back in (False, True):
                snap = now if back else snaps - 1 - now
                sign = 1.0 if back else -1.0
                pair = []
                for odd in range(2):
                    u = flow_of(snap, 0, odd) * sign
                    v = flow_of(snap, 1, odd) * sign
                    up, un = jnp.maximum(u, 0.0), jnp.minimum(u, 0.0)
                    if odd:
                        un = jnp.where(row == deep - 1, 0.0, un)
                    else:
                        up = jnp.where(row == 0, 0.0, up)
                    vp = jnp.where(first_col, 0.0, jnp.maximum(v, 0.0))
                    vn = jnp.where(last_col, 0.0, jnp.minimum(v, 0.0))
                    own = 1.0 - (up - un) - (vp - vn)
                    pair.append((own, up, un, vp, vn, u, v))
                weights.append(pair)
        for k in range(2):
            for comp in range(2):
                even, odd = disp[k][comp]
                above = (pltpu.roll(odd, 1, 0), even)
                below = (odd, pltpu.roll(even, deep - 1, 0))
                fresh = []
                for parity, d in enumerate((even, odd)):
                    own, up, un, vp, vn, u, v = weights[k][parity]
                    new = (
                        own * d
                        + up * above[parity]
                        - un * below[parity]
                        + vp * pltpu.roll(d, 1, 1)
                        - vn * pltpu.roll(d, cols - 1, 1)
                        - (u, v)[comp]
                    )
                    fresh.append(jnp.where(step < count, new, d))
                disp[k][comp] = fresh
    half = cols // 2
    tiles = [d for pair in disp for plane in pair for d in plane]
    lane = lax.broadcasted_iota(jnp.int32, (deep, LANES), 1)
    core = me_ref[0] % 2
    for side in range(2):
        at = half if side == 0 else half - LANES
        shift = 0 if side == 0 else RADIUS
        halo = jnp.zeros((deep, LANES), F32)
        for k, d in enumerate(tiles):
            turn = (k * RADIUS + shift) % LANES
            edge = d[:, at : at + LANES]
            edge = pltpu.roll(edge, turn, 1) if turn else edge
            halo = jnp.where((lane >= k * RADIUS) & (lane < (k + 1) * RADIUS), edge, halo)

        def write(ref):
            for piece in range(half // LANES):
                start = side * half + piece * LANES
                for k, d in enumerate(tiles):
                    place = (piece * len(tiles) + k) * deep
                    ref[place : place + deep] = d[:, start : start + LANES]
            ref[half // LANES * len(tiles) * deep :] = halo

        @pl.when(core == side)
        def _():
            write(near_ref)

        @pl.when(core != side)
        def _():
            write(far_ref)


def hats(offset):
    hat = jnp.maximum(RADIUS + 1 - jnp.abs(offset), 0)
    return hat.astype(BF16), (hat * offset).astype(BF16)


def split(x):
    high = x.astype(BF16)
    return high, (x - high.astype(F32)).astype(BF16)


def dot(a, b):
    return jnp.dot(a, b, preferred_element_type=F32)


def make_tables(core, rows, half, cols_ref, rows_ref):
    wide = half + LANES
    source = lax.broadcasted_iota(jnp.int32, (wide, half), 0)
    target = lax.broadcasted_iota(jnp.int32, (wide, half), 1)
    beside = source - half
    halo = jnp.where(core == 0, source, beside - RADIUS)
    offset = jnp.where(source < half, source, halo) - target
    offset = jnp.where(beside < RADIUS, offset, RADIUS + 1)
    smooth, slope = hats(offset)
    cols_ref[:, :half] = smooth
    cols_ref[:, half:] = slope
    tall = 4 * rows
    above = lax.broadcasted_iota(jnp.int32, (tall, tall), 0)
    below = lax.broadcasted_iota(jnp.int32, (tall, tall), 1)
    deep = rows // 2

    def natural(place):
        return place % deep * 2 + place % rows // deep

    offset = jnp.where(above // rows == below // rows, natural(below) - natural(above), RADIUS + 1)
    smooth, slope = hats(offset)
    for part in range(2):
        rows_ref[0, :, part * tall : (part + 1) * tall] = smooth
        rows_ref[1, :, part * tall : (part + 1) * tall] = slope


def states(parcel_refs, table, rows_ref):
    half = table.shape[1] // 2
    tall = rows_ref.shape[1]
    rows = tall // 4
    bodies, wide = [], []
    for ref in parcel_refs:
        body = [ref[k * tall : (k + 1) * tall] for k in range(half // LANES)]
        packed = ref[half // LANES * tall :]
        halo = [packed]
        for k in range(1, tall // TILE):
            halo.append(pltpu.roll(packed, LANES - k * RADIUS, 1))
        bodies.append(jnp.concatenate(body, axis=1))
        wide.append(jnp.concatenate([*body, jnp.concatenate(halo, axis=0)], axis=1))
    many = len(wide) * tall
    along = dot(jnp.concatenate(split(jnp.concatenate(wide, axis=0)), axis=0), table)
    along = along[:many] + along[many:]
    smooth, slope = rows_ref[0], rows_ref[1]
    total = sum(RADIUS + 1 - abs(o) for o in range(-RADIUS, RADIUS + 1))
    moment = sum((RADIUS + 1 - abs(o)) * o * o for o in range(-RADIUS, RADIUS + 1))
    scale = 1.0 / (total * moment)
    result = []
    for k, body in enumerate(bodies):
        parts = jnp.concatenate(split(along[k * tall : (k + 1) * tall]), axis=0)
        grad_x = dot(slope, parts[:, :half]) * scale
        grad_y = dot(smooth, parts[:, half:]) * scale
        maps = []
        for direction in range(2):
            one = slice(2 * direction * rows, (2 * direction + 1) * rows)
            two = slice((2 * direction + 1) * rows, (2 * direction + 2) * rows)
            maps.append([1.0 + grad_x[one], grad_y[one], grad_x[two], 1.0 + grad_y[two], body[one], body[two]])
        result.append(maps)
    return result


def chip_kernel(me_ref, own_ref, next_ref, inner_ref, cols_ref, rows_ref):
    core = me_ref[0] % 2
    rows, half = inner_ref.shape[3:]
    make_tables(core, rows, half, cols_ref, rows_ref)
    own, other = states((own_ref, next_ref), cols_ref[...], rows_ref)
    first = core == 0
    a, b = pick(first, own[0], other[0]), pick(first, other[0], own[0])
    put(inner_ref, a, 0, 0)
    put(inner_ref, join(a, b), 1, 0)
    a, b = pick(first, own[1], other[1]), pick(first, other[1], own[1])
    put(inner_ref, b, 1, 1)
    put(inner_ref, join(b, a), 0, 1)


def next_kernel(parcel_ref, cols_ref, rows_ref, state_ref):
    for direction, state in enumerate(states((parcel_ref,), cols_ref[...], rows_ref)[0]):
        put(state_ref, state, direction)


def slab_kernel(me_ref, inner_ref, straight_ref, across_ref, cols_ref, rows_ref, urgent_ref, other_ref, outer_ref):
    me = me_ref[0]
    first = me % 2 == 0
    lower = me // 2 % 2 == 0
    straight = planes(straight_ref, 0), planes(straight_ref, 1)
    across = states((across_ref,), cols_ref[...], rows_ref)[0]
    beside_fwd = join_ordered(first, straight[0], across[0])
    beside_bwd = join_ordered(first, across[1], straight[1])
    total_fwd = join_ordered(lower, planes(inner_ref, 1, 0), beside_fwd)
    total_bwd = join_ordered(lower, beside_bwd, planes(inner_ref, 0, 1))
    ident = identity(total_fwd[0].shape)
    put(outer_ref, pick(lower, ident, beside_fwd), 0)
    put(outer_ref, pick(lower, beside_bwd, ident), 1)
    forward = me // 8 % 2 == 0
    put(urgent_ref, pick(forward, total_fwd, total_bwd))
    put(other_ref, pick(forward, total_bwd, total_fwd))


def level_kernel(level, me_ref, urgent_ref, other_ref, outer_ref, got_urgent_ref, got_other_ref, *out_refs):
    next_urgent_ref, next_other_ref, next_outer_ref = out_refs
    slab = me_ref[0] // 4
    lower = slab // 2**level % 2 == 0
    forward = slab // 2 ** (level + 1) % 2 == 0
    urgent, other = planes(urgent_ref), planes(other_ref)
    got_urgent, got_other = planes(got_urgent_ref), planes(got_other_ref)
    fwd, bwd = pick(forward, urgent, other), pick(forward, other, urgent)
    got_fwd, got_bwd = pick(forward, got_urgent, got_other), pick(forward, got_other, got_urgent)
    outer_fwd, outer_bwd = planes(outer_ref, 0), planes(outer_ref, 1)
    put(next_outer_ref, pick(lower, outer_fwd, join(got_fwd, outer_fwd)), 0)
    put(next_outer_ref, pick(lower, join(got_bwd, outer_bwd), outer_bwd), 1)
    fwd, bwd = join_ordered(lower, fwd, got_fwd), join_ordered(lower, got_bwd, bwd)
    forward = slab // 2 ** (level + 2) % 2 == 0
    put(next_urgent_ref, pick(forward, fwd, bwd))
    put(next_other_ref, pick(forward, bwd, fwd))


def urgent_kernel(level, me_ref, urgent_ref, got_ref, out_ref):
    slab = me_ref[0] // 4
    lower = slab // 2**level % 2 == 0
    forward = slab // 2 ** (level + 1) % 2 == 0
    put(out_ref, join_ordered(lower == forward, planes(urgent_ref), planes(got_ref)))


def gather_kernel(level, me_ref, inner_ref, outer_ref, urgent_ref, other_ref, known_ref):
    me = me_ref[0]
    slab = me // 4
    lower = slab // 2**level % 2 == 0
    forward = slab // 2 ** (level + 1) % 2 == 0
    near = pick(lower == forward, planes(other_ref), planes(urgent_ref))
    before, after = planes(outer_ref, 0), planes(outer_ref, 1)
    before = pick(lower, before, join(near, before))
    after = pick(lower, join(near, after), after)
    for flip in range(2):
        window = me % 2 ^ flip
        put(known_ref, join(before, planes(inner_ref, window, 0)), flip, 0)
        put(known_ref, join(after, planes(inner_ref, window, 1)), flip, 1)


def finish(forward, known_ref, last_ref, flip, out_ref):
    fwd, bwd = planes(known_ref, flip, 0), planes(known_ref, flip, 1)
    whole = join(planes(last_ref), pick(forward, bwd, fwd))
    fwd, bwd = pick(forward, fwd, whole), pick(forward, whole, bwd)
    deep = out_ref.shape[2] // 2
    for k, plane in enumerate(strain(fwd) + strain(bwd) + fwd[4:] + bwd[4:]):
        for piece in range(out_ref.shape[1]):
            lanes = slice(piece * LANES, (piece + 1) * LANES)
            out_ref[k, piece, pl.ds(0, deep, stride=2), :] = plane[:deep, lanes]
            out_ref[k, piece, pl.ds(1, deep, stride=2), :] = plane[deep:, lanes]


def place(source, side, out_refs, sems):
    copies = []
    pieces = source.shape[1]
    for piece in range(pieces):
        at = pl.multiple_of((side * pieces + piece) * LANES, LANES)
        start = 0
        for ref in out_refs:
            many = ref.shape[1]
            target = ref.at[0, :, :, pl.ds(at, LANES)]
            copies.append(
                pltpu.make_async_copy(source.at[start : start + many, piece], target, sems.at[len(copies)])
            )
            start += many
    for copy in copies:
        copy.start()
    for copy in copies:
        copy.wait()


def theirs_kernel(level, me_ref, known_ref, last_ref, theirs_ref):
    forward = me_ref[0] // 4 // 2 ** (level + 1) % 2 == 0
    finish(forward, known_ref, last_ref, 1, theirs_ref)


def mine_kernel(level, me_ref, known_ref, last_ref, *refs):
    *out_refs, mine_ref, sems = refs
    forward = me_ref[0] // 4 // 2 ** (level + 1) % 2 == 0
    finish(forward, known_ref, last_ref, 0, mine_ref)
    place(mine_ref, me_ref[0] % 2, out_refs, sems)


def place_kernel(me_ref, theirs_ref, *refs):
    *out_refs, sems = refs[4:]
    place(theirs_ref, 1 - me_ref[0] % 2, out_refs, sems)


SMEM = pl.BlockSpec(memory_space=pltpu.SMEM)
VMEM = pl.BlockSpec(memory_space=pltpu.VMEM)
HBM = pl.BlockSpec(memory_space=pltpu.HBM)
PARAMS = pltpu.CompilerParams(vmem_limit_bytes=8 * 1024 * 1024)


def sds(*shape, dtype=F32):
    return jax.ShapeDtypeStruct(shape, dtype)


def call(kernel, outs, *args, specs=None, out_specs=None, scratch=(), aliases=None):
    specs = specs or [SMEM] * (args[0].ndim == 1) + [VMEM] * (len(args) - (args[0].ndim == 1))
    many = isinstance(outs, tuple)
    out_specs = out_specs or ((VMEM,) * len(outs) if many else VMEM)
    return pl.pallas_call(
        kernel,
        out_shape=outs,
        in_specs=specs,
        out_specs=out_specs,
        scratch_shapes=scratch,
        input_output_aliases=aliases or {},
        compiler_params=PARAMS,
    )(*args)


def shards(velocity, substep_count, sea_mask, *, windows):
    rows, cols = sea_mask.shape
    half = cols // 2
    slabs = windows // 4
    last_level = slabs.bit_length() - 2
    me = lax.axis_index("tm").astype(jnp.int32)[None]

    def swap(x, d, keep=lambda i: True):
        return lax.ppermute(x, "tm", [(i, i ^ d) for i in range(windows) if keep(i)])

    tall = 4 * rows * (half // LANES) + TILE
    near, far = call(
        advance_kernel,
        (sds(tall, LANES), sds(tall, LANES)),
        me,
        substep_count, *(pltpu.with_memory_space_constraint(x, pltpu.HBM) for x in (velocity, sea_mask)),
        specs=[SMEM, SMEM, HBM, HBM],
        scratch=[
            pltpu.VMEM(velocity.shape, velocity.dtype),
            pltpu.VMEM(sea_mask.shape, sea_mask.dtype),
            pltpu.VMEM((*velocity.shape[1:3], cols // LANES, rows, LANES), F32),
            pltpu.SemaphoreType.DMA((2 + velocity.shape[1],)),
        ],
    )
    straight = swap(near, 2)
    across = swap(far, 3)
    next_core = swap(far, 1)
    one, both = sds(6, rows, half), sds(2, 6, rows, half)
    inner, col_table, row_table = call(
        chip_kernel,
        (
            sds(2, 2, 6, rows, half),
            sds(half + LANES, cols, dtype=BF16),
            sds(2, 4 * rows, 8 * rows, dtype=BF16),
        ),
        me,
        near,
        next_core,
    )
    straight = call(next_kernel, both, straight, col_table, row_table)
    urgent, other, outer = call(
        slab_kernel, (one, one, both), me, inner, straight, across, col_table, row_table
    )
    for level in range(last_level - 1):
        urgent, other, outer = call(
            functools.partial(level_kernel, level),
            (one, one, both),
            me,
            urgent,
            other,
            outer,
            swap(urgent, 4 << level),
            swap(other, 4 << level),
        )
    level = last_level - 1

    def sends_other(i):
        return (i // 4 >> level) % 2 != (i // 4 >> last_level) % 2

    got_urgent = swap(urgent, 4 << level)
    got_other = swap(other, 4 << level)
    urgent = call(functools.partial(urgent_kernel, level), one, me, urgent, got_urgent)
    last = swap(urgent, 4 << last_level)
    known = call(
        functools.partial(gather_kernel, level), sds(2, 2, 6, rows, half), me, inner, outer, got_urgent, got_other
    )
    ten = sds(10, half // LANES, rows, LANES)
    theirs = call(functools.partial(theirs_kernel, level), ten, me, known, last)
    theirs = swap(theirs, 1)
    outs = (sds(1, 3, rows, cols), sds(1, 3, rows, cols), sds(1, 2, rows, cols), sds(1, 2, rows, cols))
    copies = pltpu.SemaphoreType.DMA((4 * (half // LANES),))
    halves = call(
        functools.partial(mine_kernel, level),
        outs,
        me,
        known,
        last,
        out_specs=(HBM,) * 4,
        scratch=[pltpu.VMEM(ten.shape, F32), copies],
    )
    return call(
        place_kernel,
        outs,
        me,
        theirs,
        *halves,
        specs=[SMEM, VMEM] + [HBM] * 4,
        out_specs=(HBM,) * 4,
        scratch=[copies],
        aliases={2 + k: k for k in range(4)},
    )


def solution(mesh):
    return jax.shard_map(
        functools.partial(shards, windows=mesh.shape["tm"]),
        mesh=mesh,
        in_specs=(P("tm", None, None, "groups", None), P("tm"), P("groups", None)),
        out_specs=(P("tm", None, "groups", None),) * 4,
        check_vma=False,
    )
```

```python
import functools

import jax
import jax.numpy as jnp
from jax import lax
from jax.experimental import pallas as pl
from jax.experimental.pallas import tpu as pltpu
from jax.sharding import PartitionSpec as P

SUBSTEPS = 12
RADIUS = 4
LANES = 128
TILE = 8
F32 = jnp.float32
BF16 = jnp.bfloat16


def join(first, then):
    e0, e1, e2, e3, e4, e5 = first
    l0, l1, l2, l3, l4, l5 = then
    return [
        l0 * e0 + l1 * e2,
        l0 * e1 + l1 * e3,
        l2 * e0 + l3 * e2,
        l2 * e1 + l3 * e3,
        l4 + l0 * e4 + l1 * e5,
        l5 + l2 * e4 + l3 * e5,
    ]


def pick(flag, yes, no):
    return [jnp.where(flag, a, b) for a, b in zip(yes, no)]


def join_ordered(flag, a, b):
    return join(pick(flag, a, b), pick(flag, b, a))


def strain(s):
    a11, a12, a21, a22, _, _ = s
    return [a11 * a11 + a21 * a21, a11 * a12 + a21 * a22, a12 * a12 + a22 * a22]


def planes(ref, *at):
    return [ref[(*at, k)] for k in range(6)]


def put(ref, values, *at):
    for k, value in enumerate(values):
        ref[(*at, k)] = value


def identity(shape):
    zero, one = jnp.zeros(shape, F32), jnp.ones(shape, F32)
    return [one, zero, zero, one, zero, zero]


def advance_kernel(me_ref, count_ref, vel_hbm, sea_hbm, near_ref, far_ref, vel_ref, sea_ref, flow_ref, sems):
    snaps, _, rows, cols = vel_ref.shape[1:]
    wait_for = [
        pltpu.make_async_copy(vel_hbm.at[0, snap], vel_ref.at[0, snap], sems.at[2 + snap]) for snap in range(snaps)
    ]
    load_sea = pltpu.make_async_copy(sea_hbm, sea_ref, sems.at[0])
    load_sea.start()
    for now in range(snaps // 2):
        wait_for[now].start()
        wait_for[snaps - 1 - now].start()
    load_sea.wait()
    per_snap = SUBSTEPS // snaps
    count = count_ref[0]
    sea = sea_ref[...].astype(F32)

    def flow_in(snap):
        wait_for[snap].wait()
        for comp in range(2):
            flow = vel_ref[0, snap, comp].astype(F32) * sea
            for piece in range(cols // LANES):
                flow_ref[snap, comp, piece] = flow[:, piece * LANES : (piece + 1) * LANES]

    deep = rows // 2

    def flow_of(snap, comp, odd):
        pieces = [flow_ref[snap, comp, piece, pl.ds(odd, deep, stride=2), :] for piece in range(cols // LANES)]
        return jnp.concatenate(pieces, axis=1)

    row = lax.broadcasted_iota(jnp.int32, (deep, cols), 0)
    col = lax.broadcasted_iota(jnp.int32, (deep, cols), 1)
    first_col, last_col = col == 0, col == cols - 1
    zero = jnp.zeros((deep, cols), F32)
    disp = [[[zero, zero], [zero, zero]], [[zero, zero], [zero, zero]]]
    for step in range(SUBSTEPS):
        if step % per_snap == 0:
            now = step // per_snap
            if now < snaps // 2:
                flow_in(now)
                flow_in(snaps - 1 - now)
            weights = []
            for back in (False, True):
                snap = now if back else snaps - 1 - now
                sign = 1.0 if back else -1.0
                pair = []
                for odd in range(2):
                    u = flow_of(snap, 0, odd) * sign
                    v = flow_of(snap, 1, odd) * sign
                    up, un = jnp.maximum(u, 0.0), jnp.minimum(u, 0.0)
                    if odd:
                        un = jnp.where(row == deep - 1, 0.0, un)
                    else:
                        up = jnp.where(row == 0, 0.0, up)
                    vp = jnp.where(first_col, 0.0, jnp.maximum(v, 0.0))
                    vn = jnp.where(last_col, 0.0, jnp.minimum(v, 0.0))
                    own = 1.0 - (up - un) - (vp - vn)
                    pair.append((own, up, un, vp, vn, u, v))
                weights.append(pair)
        for k in range(2):
            if step == 0:
                for comp in range(2):
                    disp[k][comp] = [jnp.where(count > 0, -weights[k][odd][5 + comp], 0.0) for odd in range(2)]
                continue
            for comp in range(2):
                even, odd = disp[k][comp]
                above = (pltpu.roll(odd, 1, 0), even)
                below = (odd, pltpu.roll(even, deep - 1, 0))
                fresh = []
                for parity, d in enumerate((even, odd)):
                    own, up, un, vp, vn, u, v = weights[k][parity]
                    new = (
                        (own * d - (u, v)[comp])
                        + (up * above[parity] - un * below[parity])
                        + (vp * pltpu.roll(d, 1, 1) - vn * pltpu.roll(d, cols - 1, 1))
                    )
                    fresh.append(jnp.where(step < count, new, d))
                disp[k][comp] = fresh
    half = cols // 2
    tiles = [d for pair in disp for plane in pair for d in plane]
    lane = lax.broadcasted_iota(jnp.int32, (deep, LANES), 1)
    core = me_ref[0] % 2
    for side in range(2):
        at = half if side == 0 else half - LANES
        shift = 0 if side == 0 else RADIUS
        halo = jnp.zeros((deep, LANES), F32)
        for k, d in enumerate(tiles):
            turn = (k * RADIUS + shift) % LANES
            edge = d[:, at : at + LANES]
            edge = pltpu.roll(edge, turn, 1) if turn else edge
            halo = jnp.where((lane >= k * RADIUS) & (lane < (k + 1) * RADIUS), edge, halo)

        def write(ref):
            for piece in range(half // LANES):
                start = side * half + piece * LANES
                for k, d in enumerate(tiles):
                    place = (piece * len(tiles) + k) * deep
                    ref[place : place + deep] = d[:, start : start + LANES]
            ref[half // LANES * len(tiles) * deep :] = halo

        @pl.when(core == side)
        def _():
            write(near_ref)

        @pl.when(core != side)
        def _():
            write(far_ref)


def hats(offset):
    hat = jnp.maximum(RADIUS + 1 - jnp.abs(offset), 0)
    return hat.astype(BF16), (hat * offset).astype(BF16)


def split(x):
    high = x.astype(BF16)
    return high, (x - high.astype(F32)).astype(BF16)


def dot(a, b):
    return jnp.dot(a, b, preferred_element_type=F32)


def make_tables(core, rows, half, cols_ref, rows_ref):
    wide = half + LANES
    source = lax.broadcasted_iota(jnp.int32, (wide, half), 0)
    target = lax.broadcasted_iota(jnp.int32, (wide, half), 1)
    beside = source - half
    halo = jnp.where(core == 0, source, beside - RADIUS)
    offset = jnp.where(source < half, source, halo) - target
    offset = jnp.where(beside < RADIUS, offset, RADIUS + 1)
    smooth, slope = hats(offset)
    cols_ref[:, :half] = smooth
    cols_ref[:, half:] = slope
    tall = 4 * rows
    above = lax.broadcasted_iota(jnp.int32, (tall, tall), 0)
    below = lax.broadcasted_iota(jnp.int32, (tall, tall), 1)
    deep = rows // 2

    def natural(place):
        return place % deep * 2 + place % rows // deep

    offset = jnp.where(above // rows == below // rows, natural(below) - natural(above), RADIUS + 1)
    smooth, slope = hats(offset)
    for part in range(2):
        rows_ref[0, :, part * tall : (part + 1) * tall] = smooth
        rows_ref[1, :, part * tall : (part + 1) * tall] = slope


def states(parcel_refs, table, rows_ref):
    half = table.shape[1] // 2
    tall = rows_ref.shape[1]
    rows = tall // 4
    bodies, wide = [], []
    for ref in parcel_refs:
        body = [ref[k * tall : (k + 1) * tall] for k in range(half // LANES)]
        packed = ref[half // LANES * tall :]
        halo = [packed]
        for k in range(1, tall // TILE):
            halo.append(pltpu.roll(packed, LANES - k * RADIUS, 1))
        bodies.append(jnp.concatenate(body, axis=1))
        wide.append(jnp.concatenate([*body, jnp.concatenate(halo, axis=0)], axis=1))
    many = len(wide) * tall
    along = dot(jnp.concatenate(split(jnp.concatenate(wide, axis=0)), axis=0), table)
    along = along[:many] + along[many:]
    smooth, slope = rows_ref[0], rows_ref[1]
    total = sum(RADIUS + 1 - abs(o) for o in range(-RADIUS, RADIUS + 1))
    moment = sum((RADIUS + 1 - abs(o)) * o * o for o in range(-RADIUS, RADIUS + 1))
    scale = 1.0 / (total * moment)
    result = []
    for k, body in enumerate(bodies):
        parts = jnp.concatenate(split(along[k * tall : (k + 1) * tall]), axis=0)
        grad_x = dot(slope, parts[:, :half]) * scale
        grad_y = dot(smooth, parts[:, half:]) * scale
        maps = []
        for direction in range(2):
            one = slice(2 * direction * rows, (2 * direction + 1) * rows)
            two = slice((2 * direction + 1) * rows, (2 * direction + 2) * rows)
            maps.append([1.0 + grad_x[one], grad_y[one], grad_x[two], 1.0 + grad_y[two], body[one], body[two]])
        result.append(maps)
    return result


def chip_kernel(me_ref, own_ref, next_ref, inner_ref, cols_ref, rows_ref):
    core = me_ref[0] % 2
    rows, half = inner_ref.shape[3:]
    make_tables(core, rows, half, cols_ref, rows_ref)
    own, other = states((own_ref, next_ref), cols_ref[...], rows_ref)
    first = core == 0
    a, b = pick(first, own[0], other[0]), pick(first, other[0], own[0])
    put(inner_ref, a, 0, 0)
    put(inner_ref, join(a, b), 1, 0)
    a, b = pick(first, own[1], other[1]), pick(first, other[1], own[1])
    put(inner_ref, b, 1, 1)
    put(inner_ref, join(b, a), 0, 1)


def next_kernel(parcel_ref, cols_ref, rows_ref, state_ref):
    for direction, state in enumerate(states((parcel_ref,), cols_ref[...], rows_ref)[0]):
        put(state_ref, state, direction)


def slab_totals(me_ref, directions, inner_ref, straight, across):
    me = me_ref[0]
    first = me % 2 == 0
    lower = me // 2 % 2 == 0
    result = []
    for forward, chip, near, far in zip(directions, inner_ref, straight, across):
        beside = join_ordered(first == forward, near, far)
        result.append((join_ordered(lower == forward, chip, beside), beside))
    return result


def urgent_slab_kernel(me_ref, inner_ref, straight_ref, across_ref, cols_ref, rows_ref, urgent_ref):
    forward = me_ref[0] // 8 % 2 == 0
    straight = pick(forward, planes(straight_ref, 0), planes(straight_ref, 1))
    across = pick(forward, *states((across_ref,), cols_ref[...], rows_ref)[0])
    inner = pick(forward, planes(inner_ref, 1, 0), planes(inner_ref, 0, 1))
    ((total, _),) = slab_totals(me_ref, (forward,), (inner,), (straight,), (across,))
    put(urgent_ref, total)


def slab_kernel(me_ref, inner_ref, straight_ref, across_ref, cols_ref, rows_ref, other_ref, outer_ref):
    me = me_ref[0]
    lower = me // 2 % 2 == 0
    forward = me // 8 % 2 == 0
    straight = planes(straight_ref, 0), planes(straight_ref, 1)
    across = states((across_ref,), cols_ref[...], rows_ref)[0]
    inner = planes(inner_ref, 1, 0), planes(inner_ref, 0, 1)
    fwd, bwd = slab_totals(me_ref, (True, False), inner, straight, across)
    ident = identity(fwd[0][0].shape)
    put(outer_ref, pick(lower, ident, fwd[1]), 0)
    put(outer_ref, pick(lower, bwd[1], ident), 1)
    put(other_ref, pick(forward, bwd[0], fwd[0]))


def level_kernel(level, me_ref, urgent_ref, other_ref, outer_ref, got_urgent_ref, got_other_ref, *out_refs):
    next_urgent_ref, next_other_ref, next_outer_ref = out_refs
    slab = me_ref[0] // 4
    lower = slab // 2**level % 2 == 0
    forward = slab // 2 ** (level + 1) % 2 == 0
    urgent, other = planes(urgent_ref), planes(other_ref)
    got_urgent, got_other = planes(got_urgent_ref), planes(got_other_ref)
    fwd, bwd = pick(forward, urgent, other), pick(forward, other, urgent)
    got_fwd, got_bwd = pick(forward, got_urgent, got_other), pick(forward, got_other, got_urgent)
    outer_fwd, outer_bwd = planes(outer_ref, 0), planes(outer_ref, 1)
    put(next_outer_ref, pick(lower, outer_fwd, join(got_fwd, outer_fwd)), 0)
    put(next_outer_ref, pick(lower, join(got_bwd, outer_bwd), outer_bwd), 1)
    fwd, bwd = join_ordered(lower, fwd, got_fwd), join_ordered(lower, got_bwd, bwd)
    forward = slab // 2 ** (level + 2) % 2 == 0
    put(next_urgent_ref, pick(forward, fwd, bwd))
    put(next_other_ref, pick(forward, bwd, fwd))


def urgent_kernel(level, me_ref, urgent_ref, got_ref, out_ref):
    slab = me_ref[0] // 4
    lower = slab // 2**level % 2 == 0
    forward = slab // 2 ** (level + 1) % 2 == 0
    put(out_ref, join_ordered(lower == forward, planes(urgent_ref), planes(got_ref)))


def gather_kernel(level, me_ref, inner_ref, outer_ref, urgent_ref, other_ref, known_ref):
    me = me_ref[0]
    slab = me // 4
    lower = slab // 2**level % 2 == 0
    forward = slab // 2 ** (level + 1) % 2 == 0
    near = pick(lower == forward, planes(other_ref), planes(urgent_ref))
    before, after = planes(outer_ref, 0), planes(outer_ref, 1)
    before = pick(lower, before, join(near, before))
    after = pick(lower, join(near, after), after)
    for flip in range(2):
        window = me % 2 ^ flip
        put(known_ref, join(before, planes(inner_ref, window, 0)), flip, 0)
        put(known_ref, join(after, planes(inner_ref, window, 1)), flip, 1)


def finish(forward, known_ref, last_ref, flip, out_ref):
    fwd, bwd = planes(known_ref, flip, 0), planes(known_ref, flip, 1)
    whole = join(planes(last_ref), pick(forward, bwd, fwd))
    fwd, bwd = pick(forward, fwd, whole), pick(forward, whole, bwd)
    deep = out_ref.shape[2] // 2
    for k, plane in enumerate(strain(fwd) + strain(bwd) + fwd[4:] + bwd[4:]):
        for piece in range(out_ref.shape[1]):
            lanes = slice(piece * LANES, (piece + 1) * LANES)
            out_ref[k, piece, pl.ds(0, deep, stride=2), :] = plane[:deep, lanes]
            out_ref[k, piece, pl.ds(1, deep, stride=2), :] = plane[deep:, lanes]


def place(source, side, out_refs, sems):
    copies = []
    pieces = source.shape[1]
    for piece in range(pieces):
        at = pl.multiple_of((side * pieces + piece) * LANES, LANES)
        start = 0
        for ref in out_refs:
            many = ref.shape[1]
            target = ref.at[0, :, :, pl.ds(at, LANES)]
            copies.append(
                pltpu.make_async_copy(source.at[start : start + many, piece], target, sems.at[len(copies)])
            )
            start += many
    for copy in copies:
        copy.start()
    for copy in copies:
        copy.wait()


def theirs_kernel(level, me_ref, known_ref, last_ref, theirs_ref):
    forward = me_ref[0] // 4 // 2 ** (level + 1) % 2 == 0
    finish(forward, known_ref, last_ref, 1, theirs_ref)


def mine_kernel(level, me_ref, known_ref, last_ref, *refs):
    *out_refs, mine_ref, sems = refs
    forward = me_ref[0] // 4 // 2 ** (level + 1) % 2 == 0
    finish(forward, known_ref, last_ref, 0, mine_ref)
    place(mine_ref, me_ref[0] % 2, out_refs, sems)


def place_kernel(me_ref, theirs_ref, *refs):
    *out_refs, sems = refs[4:]
    place(theirs_ref, 1 - me_ref[0] % 2, out_refs, sems)


SMEM = pl.BlockSpec(memory_space=pltpu.SMEM)
VMEM = pl.BlockSpec(memory_space=pltpu.VMEM)
HBM = pl.BlockSpec(memory_space=pltpu.HBM)
PARAMS = pltpu.CompilerParams(vmem_limit_bytes=8 * 1024 * 1024)


def sds(*shape, dtype=F32):
    return jax.ShapeDtypeStruct(shape, dtype)


def call(kernel, outs, *args, specs=None, out_specs=None, scratch=(), aliases=None):
    specs = specs or [SMEM] * (args[0].ndim == 1) + [VMEM] * (len(args) - (args[0].ndim == 1))
    many = isinstance(outs, tuple)
    out_specs = out_specs or ((VMEM,) * len(outs) if many else VMEM)
    return pl.pallas_call(
        kernel,
        out_shape=outs,
        in_specs=specs,
        out_specs=out_specs,
        scratch_shapes=scratch,
        input_output_aliases=aliases or {},
        compiler_params=PARAMS,
    )(*args)


def shards(velocity, substep_count, sea_mask, *, windows):
    rows, cols = sea_mask.shape
    half = cols // 2
    slabs = windows // 4
    last_level = slabs.bit_length() - 2
    me = lax.axis_index("tm").astype(jnp.int32)[None]

    def swap(x, d, keep=lambda i: True):
        return lax.ppermute(x, "tm", [(i, i ^ d) for i in range(windows) if keep(i)])

    tall = 4 * rows * (half // LANES) + TILE
    near, far = call(
        advance_kernel,
        (sds(tall, LANES), sds(tall, LANES)),
        me,
        substep_count, *(pltpu.with_memory_space_constraint(x, pltpu.HBM) for x in (velocity, sea_mask)),
        specs=[SMEM, SMEM, HBM, HBM],
        scratch=[
            pltpu.VMEM(velocity.shape, velocity.dtype),
            pltpu.VMEM(sea_mask.shape, sea_mask.dtype),
            pltpu.VMEM((*velocity.shape[1:3], cols // LANES, rows, LANES), F32),
            pltpu.SemaphoreType.DMA((2 + velocity.shape[1],)),
        ],
    )
    straight = swap(near, 2)
    across = swap(far, 3)
    next_core = swap(far, 1)
    one, both = sds(6, rows, half), sds(2, 6, rows, half)
    inner, col_table, row_table = call(
        chip_kernel,
        (
            sds(2, 2, 6, rows, half),
            sds(half + LANES, cols, dtype=BF16),
            sds(2, 4 * rows, 8 * rows, dtype=BF16),
        ),
        me,
        near,
        next_core,
    )
    straight = call(next_kernel, both, straight, col_table, row_table)
    urgent = call(urgent_slab_kernel, one, me, inner, straight, across, col_table, row_table)
    other, outer = call(slab_kernel, (one, both), me, inner, straight, across, col_table, row_table)
    for level in range(last_level - 1):
        urgent, other, outer = call(
            functools.partial(level_kernel, level),
            (one, one, both),
            me,
            urgent,
            other,
            outer,
            swap(urgent, 4 << level),
            swap(other, 4 << level),
        )
    level = last_level - 1

    def sends_other(i):
        return (i // 4 >> level) % 2 != (i // 4 >> last_level) % 2

    got_urgent = swap(urgent, 4 << level)
    got_other = swap(other, 4 << level)
    urgent = call(functools.partial(urgent_kernel, level), one, me, urgent, got_urgent)
    last = swap(urgent, 4 << last_level)
    known = call(
        functools.partial(gather_kernel, level), sds(2, 2, 6, rows, half), me, inner, outer, got_urgent, got_other
    )
    ten = sds(10, half // LANES, rows, LANES)
    theirs = call(functools.partial(theirs_kernel, level), ten, me, known, last)
    theirs = swap(theirs, 1)
    outs = (sds(1, 3, rows, cols), sds(1, 3, rows, cols), sds(1, 2, rows, cols), sds(1, 2, rows, cols))
    copies = pltpu.SemaphoreType.DMA((4 * (half // LANES),))
    halves = call(
        functools.partial(mine_kernel, level),
        outs,
        me,
        known,
        last,
        out_specs=(HBM,) * 4,
        scratch=[pltpu.VMEM(ten.shape, F32), copies],
    )
    return call(
        place_kernel,
        outs,
        me,
        theirs,
        *halves,
        specs=[SMEM, VMEM] + [HBM] * 4,
        out_specs=(HBM,) * 4,
        scratch=[copies],
        aliases={2 + k: k for k in range(4)},
    )


def solution(mesh):
    return jax.shard_map(
        functools.partial(shards, windows=mesh.shape["tm"]),
        mesh=mesh,
        in_specs=(P("tm", None, None, "groups", None), P("tm"), P("groups", None)),
        out_specs=(P("tm", None, "groups", None),) * 4,
        check_vma=False,
    )
```

```python
import functools

import jax
import jax.numpy as jnp
from jax import lax
from jax.experimental import pallas as pl
from jax.experimental.pallas import tpu as pltpu
from jax.sharding import PartitionSpec as P

SUBSTEPS = 12
RADIUS = 4
LANES = 128
TILE = 8
F32 = jnp.float32
BF16 = jnp.bfloat16


def join(first, then):
    e0, e1, e2, e3, e4, e5 = first
    l0, l1, l2, l3, l4, l5 = then
    return [
        l0 * e0 + l1 * e2,
        l0 * e1 + l1 * e3,
        l2 * e0 + l3 * e2,
        l2 * e1 + l3 * e3,
        l4 + l0 * e4 + l1 * e5,
        l5 + l2 * e4 + l3 * e5,
    ]


def pick(flag, yes, no):
    return [jnp.where(flag, a, b) for a, b in zip(yes, no)]


def join_ordered(flag, a, b):
    return join(pick(flag, a, b), pick(flag, b, a))


def strain(s):
    a11, a12, a21, a22, _, _ = s
    return [a11 * a11 + a21 * a21, a11 * a12 + a21 * a22, a12 * a12 + a22 * a22]


def planes(ref, *at):
    return [ref[(*at, k)] for k in range(6)]


def put(ref, values, *at):
    for k, value in enumerate(values):
        ref[(*at, k)] = value


def identity(shape):
    zero, one = jnp.zeros(shape, F32), jnp.ones(shape, F32)
    return [one, zero, zero, one, zero, zero]


def advance_kernel(me_ref, count_ref, vel_hbm, sea_hbm, near_ref, far_ref, vel_ref, sea_ref, flow_ref, sems):
    snaps, _, rows, cols = vel_ref.shape[1:]
    wait_for = [
        pltpu.make_async_copy(vel_hbm.at[0, snap], vel_ref.at[0, snap], sems.at[2 + snap]) for snap in range(snaps)
    ]
    load_sea = pltpu.make_async_copy(sea_hbm, sea_ref, sems.at[0])
    load_sea.start()
    for now in range(snaps // 2):
        wait_for[now].start()
        wait_for[snaps - 1 - now].start()
    load_sea.wait()
    per_snap = SUBSTEPS // snaps
    count = count_ref[0]
    sea = sea_ref[...].astype(F32)

    def flow_in(snap):
        wait_for[snap].wait()
        for comp in range(2):
            flow = vel_ref[0, snap, comp].astype(F32) * sea
            for piece in range(cols // LANES):
                flow_ref[snap, comp, piece] = flow[:, piece * LANES : (piece + 1) * LANES]

    deep = rows // 2

    def flow_of(snap, comp, odd):
        pieces = [flow_ref[snap, comp, piece, pl.ds(odd, deep, stride=2), :] for piece in range(cols // LANES)]
        return jnp.concatenate(pieces, axis=1)

    row = lax.broadcasted_iota(jnp.int32, (deep, cols), 0)
    col = lax.broadcasted_iota(jnp.int32, (deep, cols), 1)
    first_col, last_col = col == 0, col == cols - 1
    zero = jnp.zeros((deep, cols), F32)
    disp = [[[zero, zero], [zero, zero]], [[zero, zero], [zero, zero]]]
    for step in range(SUBSTEPS):
        if step % per_snap == 0:
            now = step // per_snap
            if now < snaps // 2:
                flow_in(now)
                flow_in(snaps - 1 - now)
            weights = []
            for back in (False, True):
                snap = now if back else snaps - 1 - now
                sign = 1.0 if back else -1.0
                pair = []
                for odd in range(2):
                    u = flow_of(snap, 0, odd) * sign
                    v = flow_of(snap, 1, odd) * sign
                    up, un = jnp.maximum(u, 0.0), jnp.minimum(u, 0.0)
                    if odd:
                        un = jnp.where(row == deep - 1, 0.0, un)
                    else:
                        up = jnp.where(row == 0, 0.0, up)
                    vp = jnp.where(first_col, 0.0, jnp.maximum(v, 0.0))
                    vn = jnp.where(last_col, 0.0, jnp.minimum(v, 0.0))
                    own = 1.0 - (up - un) - (vp - vn)
                    pair.append((own, up, un, vp, vn, u, v))
                weights.append(pair)
        for k in range(2):
            if step == 0:
                for comp in range(2):
                    disp[k][comp] = [jnp.where(count > 0, -weights[k][odd][5 + comp], 0.0) for odd in range(2)]
                continue
            for comp in range(2):
                even, odd = disp[k][comp]
                above = (pltpu.roll(odd, 1, 0), even)
                below = (odd, pltpu.roll(even, deep - 1, 0))
                fresh = []
                for parity, d in enumerate((even, odd)):
                    own, up, un, vp, vn, u, v = weights[k][parity]
                    new = (
                        (own * d - (u, v)[comp])
                        + (up * above[parity] - un * below[parity])
                        + (vp * pltpu.roll(d, 1, 1) - vn * pltpu.roll(d, cols - 1, 1))
                    )
                    fresh.append(jnp.where(step < count, new, d))
                disp[k][comp] = fresh
    half = cols // 2
    tiles = [d for pair in disp for plane in pair for d in plane]
    lane = lax.broadcasted_iota(jnp.int32, (deep, LANES), 1)
    core = me_ref[0] % 2
    for side in range(2):
        at = half if side == 0 else half - LANES
        shift = 0 if side == 0 else RADIUS
        halo = jnp.zeros((deep, LANES), F32)
        for k, d in enumerate(tiles):
            turn = (k * RADIUS + shift) % LANES
            edge = d[:, at : at + LANES]
            edge = pltpu.roll(edge, turn, 1) if turn else edge
            halo = jnp.where((lane >= k * RADIUS) & (lane < (k + 1) * RADIUS), edge, halo)

        def write(ref):
            for piece in range(half // LANES):
                start = side * half + piece * LANES
                for k, d in enumerate(tiles):
                    place = (piece * len(tiles) + k) * deep
                    ref[place : place + deep] = d[:, start : start + LANES]
            ref[half // LANES * len(tiles) * deep :] = halo

        @pl.when(core == side)
        def _():
            write(near_ref)

        @pl.when(core != side)
        def _():
            write(far_ref)


def hats(offset):
    hat = jnp.maximum(RADIUS + 1 - jnp.abs(offset), 0)
    return hat.astype(BF16), (hat * offset).astype(BF16)


def split(x):
    high = x.astype(BF16)
    return high, (x - high.astype(F32)).astype(BF16)


def dot(a, b):
    return jnp.dot(a, b, preferred_element_type=F32)


def make_tables(core, rows, half, cols_ref, rows_ref):
    wide = half + LANES
    source = lax.broadcasted_iota(jnp.int32, (wide, half), 0)
    target = lax.broadcasted_iota(jnp.int32, (wide, half), 1)
    beside = source - half
    halo = jnp.where(core == 0, source, beside - RADIUS)
    offset = jnp.where(source < half, source, halo) - target
    offset = jnp.where(beside < RADIUS, offset, RADIUS + 1)
    smooth, slope = hats(offset)
    cols_ref[:, :half] = smooth
    cols_ref[:, half:] = slope
    tall = 4 * rows
    above = lax.broadcasted_iota(jnp.int32, (tall, tall), 0)
    below = lax.broadcasted_iota(jnp.int32, (tall, tall), 1)
    deep = rows // 2

    def natural(place):
        return place % deep * 2 + place % rows // deep

    offset = jnp.where(above // rows == below // rows, natural(below) - natural(above), RADIUS + 1)
    smooth, slope = hats(offset)
    for part in range(2):
        rows_ref[0, :, part * tall : (part + 1) * tall] = smooth
        rows_ref[1, :, part * tall : (part + 1) * tall] = slope


def states(parcel_refs, table, rows_ref):
    half = table.shape[1] // 2
    tall = rows_ref.shape[1]
    rows = tall // 4
    bodies, wide = [], []
    for ref in parcel_refs:
        body = [ref[k * tall : (k + 1) * tall] for k in range(half // LANES)]
        packed = ref[half // LANES * tall :]
        halo = [packed]
        for k in range(1, tall // TILE):
            halo.append(pltpu.roll(packed, LANES - k * RADIUS, 1))
        bodies.append(jnp.concatenate(body, axis=1))
        wide.append(jnp.concatenate([*body, jnp.concatenate(halo, axis=0)], axis=1))
    total = sum(RADIUS + 1 - abs(o) for o in range(-RADIUS, RADIUS + 1))
    moment = sum((RADIUS + 1 - abs(o)) * o * o for o in range(-RADIUS, RADIUS + 1))
    scale = 1.0 / (total * moment)
    result = []
    weights = rows_ref[...].reshape(2 * tall, 2 * tall)
    for body, values in zip(bodies, wide):
        mixed = dot(weights, jnp.concatenate(split(values), axis=0))
        grad_x = dot(jnp.concatenate(split(mixed[tall:]), axis=0), table[:, :half])
        grad_y = dot(jnp.concatenate(split(mixed[:tall]), axis=0), table[:, half:])
        grad_x = (grad_x[:tall] + grad_x[tall:]) * scale
        grad_y = (grad_y[:tall] + grad_y[tall:]) * scale
        maps = []
        for direction in range(2):
            one = slice(2 * direction * rows, (2 * direction + 1) * rows)
            two = slice((2 * direction + 1) * rows, (2 * direction + 2) * rows)
            maps.append([1.0 + grad_x[one], grad_y[one], grad_x[two], 1.0 + grad_y[two], body[one], body[two]])
        result.append(maps)
    return result


def chip_kernel(me_ref, own_ref, next_ref, inner_ref, cols_ref, rows_ref):
    core = me_ref[0] % 2
    rows, half = inner_ref.shape[3:]
    make_tables(core, rows, half, cols_ref, rows_ref)
    own, other = states((own_ref, next_ref), cols_ref[...], rows_ref)
    first = core == 0
    a, b = pick(first, own[0], other[0]), pick(first, other[0], own[0])
    put(inner_ref, a, 0, 0)
    put(inner_ref, join(a, b), 1, 0)
    a, b = pick(first, own[1], other[1]), pick(first, other[1], own[1])
    put(inner_ref, b, 1, 1)
    put(inner_ref, join(b, a), 0, 1)


def next_kernel(parcel_ref, cols_ref, rows_ref, state_ref):
    for direction, state in enumerate(states((parcel_ref,), cols_ref[...], rows_ref)[0]):
        put(state_ref, state, direction)


def slab_totals(me_ref, directions, inner_ref, straight, across):
    me = me_ref[0]
    first = me % 2 == 0
    lower = me // 2 % 2 == 0
    result = []
    for forward, chip, near, far in zip(directions, inner_ref, straight, across):
        beside = join_ordered(first == forward, near, far)
        result.append((join_ordered(lower == forward, chip, beside), beside))
    return result


def urgent_slab_kernel(me_ref, inner_ref, straight_ref, across_ref, cols_ref, rows_ref, urgent_ref):
    forward = me_ref[0] // 8 % 2 == 0
    straight = pick(forward, planes(straight_ref, 0), planes(straight_ref, 1))
    across = pick(forward, *states((across_ref,), cols_ref[...], rows_ref)[0])
    inner = pick(forward, planes(inner_ref, 1, 0), planes(inner_ref, 0, 1))
    ((total, _),) = slab_totals(me_ref, (forward,), (inner,), (straight,), (across,))
    put(urgent_ref, total)


def slab_kernel(me_ref, inner_ref, straight_ref, across_ref, cols_ref, rows_ref, other_ref, outer_ref):
    me = me_ref[0]
    lower = me // 2 % 2 == 0
    forward = me // 8 % 2 == 0
    straight = planes(straight_ref, 0), planes(straight_ref, 1)
    across = states((across_ref,), cols_ref[...], rows_ref)[0]
    inner = planes(inner_ref, 1, 0), planes(inner_ref, 0, 1)
    fwd, bwd = slab_totals(me_ref, (True, False), inner, straight, across)
    ident = identity(fwd[0][0].shape)
    put(outer_ref, pick(lower, ident, fwd[1]), 0)
    put(outer_ref, pick(lower, bwd[1], ident), 1)
    put(other_ref, pick(forward, bwd[0], fwd[0]))


def level_kernel(level, me_ref, urgent_ref, other_ref, outer_ref, got_urgent_ref, got_other_ref, *out_refs):
    next_urgent_ref, next_other_ref, next_outer_ref = out_refs
    slab = me_ref[0] // 4
    lower = slab // 2**level % 2 == 0
    forward = slab // 2 ** (level + 1) % 2 == 0
    urgent, other = planes(urgent_ref), planes(other_ref)
    got_urgent, got_other = planes(got_urgent_ref), planes(got_other_ref)
    fwd, bwd = pick(forward, urgent, other), pick(forward, other, urgent)
    got_fwd, got_bwd = pick(forward, got_urgent, got_other), pick(forward, got_other, got_urgent)
    outer_fwd, outer_bwd = planes(outer_ref, 0), planes(outer_ref, 1)
    put(next_outer_ref, pick(lower, outer_fwd, join(got_fwd, outer_fwd)), 0)
    put(next_outer_ref, pick(lower, join(got_bwd, outer_bwd), outer_bwd), 1)
    fwd, bwd = join_ordered(lower, fwd, got_fwd), join_ordered(lower, got_bwd, bwd)
    forward = slab // 2 ** (level + 2) % 2 == 0
    put(next_urgent_ref, pick(forward, fwd, bwd))
    put(next_other_ref, pick(forward, bwd, fwd))


def urgent_kernel(level, me_ref, urgent_ref, got_ref, out_ref):
    slab = me_ref[0] // 4
    lower = slab // 2**level % 2 == 0
    forward = slab // 2 ** (level + 1) % 2 == 0
    put(out_ref, join_ordered(lower == forward, planes(urgent_ref), planes(got_ref)))


def gather_kernel(level, me_ref, inner_ref, outer_ref, urgent_ref, other_ref, known_ref):
    me = me_ref[0]
    slab = me // 4
    lower = slab // 2**level % 2 == 0
    forward = slab // 2 ** (level + 1) % 2 == 0
    near = pick(lower == forward, planes(other_ref), planes(urgent_ref))
    before, after = planes(outer_ref, 0), planes(outer_ref, 1)
    before = pick(lower, before, join(near, before))
    after = pick(lower, join(near, after), after)
    for flip in range(2):
        window = me % 2 ^ flip
        put(known_ref, join(before, planes(inner_ref, window, 0)), flip, 0)
        put(known_ref, join(after, planes(inner_ref, window, 1)), flip, 1)


def finish(forward, known_ref, last_ref, flip, out_ref):
    fwd, bwd = planes(known_ref, flip, 0), planes(known_ref, flip, 1)
    whole = join(planes(last_ref), pick(forward, bwd, fwd))
    fwd, bwd = pick(forward, fwd, whole), pick(forward, whole, bwd)
    deep = out_ref.shape[2] // 2
    for k, plane in enumerate(strain(fwd) + strain(bwd) + fwd[4:] + bwd[4:]):
        for piece in range(out_ref.shape[1]):
            lanes = slice(piece * LANES, (piece + 1) * LANES)
            out_ref[k, piece, pl.ds(0, deep, stride=2), :] = plane[:deep, lanes]
            out_ref[k, piece, pl.ds(1, deep, stride=2), :] = plane[deep:, lanes]


def place(source, side, out_refs, sems):
    copies = []
    pieces = source.shape[1]
    for piece in range(pieces):
        at = pl.multiple_of((side * pieces + piece) * LANES, LANES)
        start = 0
        for ref in out_refs:
            many = ref.shape[1]
            target = ref.at[0, :, :, pl.ds(at, LANES)]
            copies.append(
                pltpu.make_async_copy(source.at[start : start + many, piece], target, sems.at[len(copies)])
            )
            start += many
    for copy in copies:
        copy.start()
    for copy in copies:
        copy.wait()


def theirs_kernel(level, me_ref, known_ref, last_ref, theirs_ref):
    forward = me_ref[0] // 4 // 2 ** (level + 1) % 2 == 0
    finish(forward, known_ref, last_ref, 1, theirs_ref)


def mine_kernel(level, me_ref, known_ref, last_ref, *refs):
    *out_refs, mine_ref, sems = refs
    forward = me_ref[0] // 4 // 2 ** (level + 1) % 2 == 0
    finish(forward, known_ref, last_ref, 0, mine_ref)
    place(mine_ref, me_ref[0] % 2, out_refs, sems)


def place_kernel(me_ref, theirs_ref, *refs):
    *out_refs, sems = refs[4:]
    place(theirs_ref, 1 - me_ref[0] % 2, out_refs, sems)


SMEM = pl.BlockSpec(memory_space=pltpu.SMEM)
VMEM = pl.BlockSpec(memory_space=pltpu.VMEM)
HBM = pl.BlockSpec(memory_space=pltpu.HBM)
PARAMS = pltpu.CompilerParams(vmem_limit_bytes=8 * 1024 * 1024)


def sds(*shape, dtype=F32):
    return jax.ShapeDtypeStruct(shape, dtype)


def call(kernel, outs, *args, specs=None, out_specs=None, scratch=(), aliases=None):
    specs = specs or [SMEM] * (args[0].ndim == 1) + [VMEM] * (len(args) - (args[0].ndim == 1))
    many = isinstance(outs, tuple)
    out_specs = out_specs or ((VMEM,) * len(outs) if many else VMEM)
    return pl.pallas_call(
        kernel,
        out_shape=outs,
        in_specs=specs,
        out_specs=out_specs,
        scratch_shapes=scratch,
        input_output_aliases=aliases or {},
        compiler_params=PARAMS,
    )(*args)


def shards(velocity, substep_count, sea_mask, *, windows):
    rows, cols = sea_mask.shape
    half = cols // 2
    slabs = windows // 4
    last_level = slabs.bit_length() - 2
    me = lax.axis_index("tm").astype(jnp.int32)[None]

    def swap(x, d, keep=lambda i: True):
        return lax.ppermute(x, "tm", [(i, i ^ d) for i in range(windows) if keep(i)])

    tall = 4 * rows * (half // LANES) + TILE
    near, far = call(
        advance_kernel,
        (sds(tall, LANES), sds(tall, LANES)),
        me,
        substep_count, *(pltpu.with_memory_space_constraint(x, pltpu.HBM) for x in (velocity, sea_mask)),
        specs=[SMEM, SMEM, HBM, HBM],
        scratch=[
            pltpu.VMEM(velocity.shape, velocity.dtype),
            pltpu.VMEM(sea_mask.shape, sea_mask.dtype),
            pltpu.VMEM((*velocity.shape[1:3], cols // LANES, rows, LANES), F32),
            pltpu.SemaphoreType.DMA((2 + velocity.shape[1],)),
        ],
    )
    straight = swap(near, 2)
    across = swap(far, 3)
    next_core = swap(far, 1)
    one, both = sds(6, rows, half), sds(2, 6, rows, half)
    inner, col_table, row_table = call(
        chip_kernel,
        (
            sds(2, 2, 6, rows, half),
            sds(half + LANES, cols, dtype=BF16),
            sds(2, 4 * rows, 8 * rows, dtype=BF16),
        ),
        me,
        near,
        next_core,
    )
    straight = call(next_kernel, both, straight, col_table, row_table)
    urgent = call(urgent_slab_kernel, one, me, inner, straight, across, col_table, row_table)
    other, outer = call(slab_kernel, (one, both), me, inner, straight, across, col_table, row_table)
    for level in range(last_level - 1):
        urgent, other, outer = call(
            functools.partial(level_kernel, level),
            (one, one, both),
            me,
            urgent,
            other,
            outer,
            swap(urgent, 4 << level),
            swap(other, 4 << level),
        )
    level = last_level - 1

    def sends_other(i):
        return (i // 4 >> level) % 2 != (i // 4 >> last_level) % 2

    got_urgent = swap(urgent, 4 << level)
    got_other = swap(other, 4 << level)
    urgent = call(functools.partial(urgent_kernel, level), one, me, urgent, got_urgent)
    last = swap(urgent, 4 << last_level)
    known = call(
        functools.partial(gather_kernel, level), sds(2, 2, 6, rows, half), me, inner, outer, got_urgent, got_other
    )
    ten = sds(10, half // LANES, rows, LANES)
    theirs = call(functools.partial(theirs_kernel, level), ten, me, known, last)
    theirs = swap(theirs, 1)
    outs = (sds(1, 3, rows, cols), sds(1, 3, rows, cols), sds(1, 2, rows, cols), sds(1, 2, rows, cols))
    copies = pltpu.SemaphoreType.DMA((4 * (half // LANES),))
    halves = call(
        functools.partial(mine_kernel, level),
        outs,
        me,
        known,
        last,
        out_specs=(HBM,) * 4,
        scratch=[pltpu.VMEM(ten.shape, F32), copies],
    )
    return call(
        place_kernel,
        outs,
        me,
        theirs,
        *halves,
        specs=[SMEM, VMEM] + [HBM] * 4,
        out_specs=(HBM,) * 4,
        scratch=[copies],
        aliases={2 + k: k for k in range(4)},
    )


def solution(mesh):
    return jax.shard_map(
        functools.partial(shards, windows=mesh.shape["tm"]),
        mesh=mesh,
        in_specs=(P("tm", None, None, "groups", None), P("tm"), P("groups", None)),
        out_specs=(P("tm", None, "groups", None),) * 4,
        check_vma=False,
    )
```

```python
import functools

import jax
import jax.numpy as jnp
from jax import lax
from jax.experimental import pallas as pl
from jax.experimental.pallas import tpu as pltpu
from jax.sharding import PartitionSpec as P

SUBSTEPS = 12
RADIUS = 4
LANES = 128
TILE = 8
F32 = jnp.float32
BF16 = jnp.bfloat16


def join(first, then):
    e0, e1, e2, e3, e4, e5 = first
    l0, l1, l2, l3, l4, l5 = then
    return [
        l0 * e0 + l1 * e2,
        l0 * e1 + l1 * e3,
        l2 * e0 + l3 * e2,
        l2 * e1 + l3 * e3,
        l4 + l0 * e4 + l1 * e5,
        l5 + l2 * e4 + l3 * e5,
    ]


def pick(flag, yes, no):
    return [jnp.where(flag, a, b) for a, b in zip(yes, no)]


def join_ordered(flag, a, b):
    return join(pick(flag, a, b), pick(flag, b, a))


def strain(s):
    a11, a12, a21, a22, _, _ = s
    return [a11 * a11 + a21 * a21, a11 * a12 + a21 * a22, a12 * a12 + a22 * a22]


def planes(ref, *at):
    return [ref[(*at, k)] for k in range(6)]


def put(ref, values, *at):
    for k, value in enumerate(values):
        ref[(*at, k)] = value


def identity(shape):
    zero, one = jnp.zeros(shape, F32), jnp.ones(shape, F32)
    return [one, zero, zero, one, zero, zero]


def advance_kernel(me_ref, count_ref, vel_hbm, sea_hbm, near_ref, far_ref, vel_ref, sea_ref, flow_ref, sems):
    snaps, _, rows, cols = vel_ref.shape[1:]
    wait_for = [
        pltpu.make_async_copy(vel_hbm.at[0, snap], vel_ref.at[0, snap], sems.at[2 + snap]) for snap in range(snaps)
    ]
    load_sea = pltpu.make_async_copy(sea_hbm, sea_ref, sems.at[0])
    load_sea.start()
    for now in range(snaps // 2):
        wait_for[now].start()
        wait_for[snaps - 1 - now].start()
    load_sea.wait()
    per_snap = SUBSTEPS // snaps
    count = count_ref[0]
    sea = sea_ref[...].astype(F32)

    def flow_in(snap):
        wait_for[snap].wait()
        for comp in range(2):
            flow = vel_ref[0, snap, comp].astype(F32) * sea
            for piece in range(cols // LANES):
                flow_ref[snap, comp, piece] = flow[:, piece * LANES : (piece + 1) * LANES]

    deep = rows // 2

    def flow_of(snap, comp, odd):
        pieces = [flow_ref[snap, comp, piece, pl.ds(odd, deep, stride=2), :] for piece in range(cols // LANES)]
        return jnp.concatenate(pieces, axis=1)

    row = lax.broadcasted_iota(jnp.int32, (deep, cols), 0)
    col = lax.broadcasted_iota(jnp.int32, (deep, cols), 1)
    first_col, last_col = col == 0, col == cols - 1
    zero = jnp.zeros((deep, cols), F32)
    disp = [[[zero, zero], [zero, zero]], [[zero, zero], [zero, zero]]]
    for step in range(SUBSTEPS):
        if step % per_snap == 0:
            now = step // per_snap
            if now < snaps // 2:
                flow_in(now)
                flow_in(snaps - 1 - now)
            weights = []
            for back in (False, True):
                snap = now if back else snaps - 1 - now
                sign = 1.0 if back else -1.0
                pair = []
                for odd in range(2):
                    u = flow_of(snap, 0, odd) * sign
                    v = flow_of(snap, 1, odd) * sign
                    up, un = jnp.maximum(u, 0.0), jnp.minimum(u, 0.0)
                    if odd:
                        un = jnp.where(row == deep - 1, 0.0, un)
                    else:
                        up = jnp.where(row == 0, 0.0, up)
                    vp = jnp.where(first_col, 0.0, jnp.maximum(v, 0.0))
                    vn = jnp.where(last_col, 0.0, jnp.minimum(v, 0.0))
                    own = 1.0 - (up - un) - (vp - vn)
                    pair.append((own, up, un, vp, vn, u, v))
                weights.append(pair)
        for k in range(2):
            if step == 0:
                for comp in range(2):
                    disp[k][comp] = [jnp.where(count > 0, -weights[k][odd][5 + comp], 0.0) for odd in range(2)]
                continue
            for comp in range(2):
                even, odd = disp[k][comp]
                above = (pltpu.roll(odd, 1, 0), even)
                below = (odd, pltpu.roll(even, deep - 1, 0))
                fresh = []
                for parity, d in enumerate((even, odd)):
                    own, up, un, vp, vn, u, v = weights[k][parity]
                    new = (
                        (own * d - (u, v)[comp])
                        + (up * above[parity] - un * below[parity])
                        + (vp * pltpu.roll(d, 1, 1) - vn * pltpu.roll(d, cols - 1, 1))
                    )
                    fresh.append(jnp.where(step < count, new, d))
                disp[k][comp] = fresh
    half = cols // 2
    tiles = [d for pair in disp for plane in pair for d in plane]
    lane = lax.broadcasted_iota(jnp.int32, (deep, LANES), 1)
    core = me_ref[0] % 2
    for side in range(2):
        at = half if side == 0 else half - LANES
        shift = 0 if side == 0 else RADIUS
        halo = jnp.zeros((deep, LANES), F32)
        for k, d in enumerate(tiles):
            turn = (k * RADIUS + shift) % LANES
            edge = d[:, at : at + LANES]
            edge = pltpu.roll(edge, turn, 1) if turn else edge
            halo = jnp.where((lane >= k * RADIUS) & (lane < (k + 1) * RADIUS), edge, halo)

        def write(ref):
            for piece in range(half // LANES):
                start = side * half + piece * LANES
                for k, d in enumerate(tiles):
                    place = (piece * len(tiles) + k) * deep
                    ref[place : place + deep] = d[:, start : start + LANES]
            ref[half // LANES * len(tiles) * deep :] = halo

        @pl.when(core == side)
        def _():
            write(near_ref)

        @pl.when(core != side)
        def _():
            write(far_ref)


def hats(offset):
    hat = jnp.maximum(RADIUS + 1 - jnp.abs(offset), 0)
    return hat.astype(BF16), (hat * offset).astype(BF16)


def split(x):
    high = x.astype(BF16)
    return high, (x - high.astype(F32)).astype(BF16)


def dot(a, b):
    return jnp.dot(a, b, preferred_element_type=F32)


def make_tables(core, rows, half, cols_ref, rows_ref):
    wide = half + LANES
    source = lax.broadcasted_iota(jnp.int32, (wide, half), 0)
    target = lax.broadcasted_iota(jnp.int32, (wide, half), 1)
    beside = source - half
    halo = jnp.where(core == 0, source, beside - RADIUS)
    offset = jnp.where(source < half, source, halo) - target
    offset = jnp.where(beside < RADIUS, offset, RADIUS + 1)
    smooth, slope = hats(offset)
    cols_ref[:, :half] = smooth
    cols_ref[:, half:] = slope
    tall = 4 * rows
    above = lax.broadcasted_iota(jnp.int32, (tall, tall), 0)
    below = lax.broadcasted_iota(jnp.int32, (tall, tall), 1)
    deep = rows // 2

    def natural(place):
        return place % deep * 2 + place % rows // deep

    offset = jnp.where(above // rows == below // rows, natural(below) - natural(above), RADIUS + 1)
    smooth, slope = hats(offset)
    for part in range(2):
        rows_ref[0, :, part * tall : (part + 1) * tall] = smooth
        rows_ref[1, :, part * tall : (part + 1) * tall] = slope


def states(parcel_refs, table, rows_ref):
    half = table.shape[1] // 2
    tall = rows_ref.shape[1]
    rows = tall // 4
    bodies, wide = [], []
    for ref in parcel_refs:
        body = [ref[k * tall : (k + 1) * tall] for k in range(half // LANES)]
        packed = ref[half // LANES * tall :]
        halo = [packed]
        for k in range(1, tall // TILE):
            halo.append(pltpu.roll(packed, LANES - k * RADIUS, 1))
        bodies.append(jnp.concatenate(body, axis=1))
        wide.append(jnp.concatenate([*body, jnp.concatenate(halo, axis=0)], axis=1))
    total = sum(RADIUS + 1 - abs(o) for o in range(-RADIUS, RADIUS + 1))
    moment = sum((RADIUS + 1 - abs(o)) * o * o for o in range(-RADIUS, RADIUS + 1))
    scale = 1.0 / (total * moment)
    result = []
    weights = rows_ref[...].reshape(2 * tall, 2 * tall)
    for body, values in zip(bodies, wide):
        mixed = dot(weights, jnp.concatenate(split(values), axis=0))
        grad_x = dot(jnp.concatenate(split(mixed[tall:]), axis=0), table[:, :half])
        grad_y = dot(jnp.concatenate(split(mixed[:tall]), axis=0), table[:, half:])
        grad_x = (grad_x[:tall] + grad_x[tall:]) * scale
        grad_y = (grad_y[:tall] + grad_y[tall:]) * scale
        maps = []
        for direction in range(2):
            one = slice(2 * direction * rows, (2 * direction + 1) * rows)
            two = slice((2 * direction + 1) * rows, (2 * direction + 2) * rows)
            maps.append([1.0 + grad_x[one], grad_y[one], grad_x[two], 1.0 + grad_y[two], body[one], body[two]])
        result.append(maps)
    return result


def chip_kernel(me_ref, own_ref, next_ref, inner_ref, cols_ref, rows_ref):
    core = me_ref[0] % 2
    rows, half = inner_ref.shape[3:]
    make_tables(core, rows, half, cols_ref, rows_ref)
    own, other = states((own_ref, next_ref), cols_ref[...], rows_ref)
    first = core == 0
    a, b = pick(first, own[0], other[0]), pick(first, other[0], own[0])
    put(inner_ref, a, 0, 0)
    put(inner_ref, join(a, b), 1, 0)
    a, b = pick(first, own[1], other[1]), pick(first, other[1], own[1])
    put(inner_ref, b, 1, 1)
    put(inner_ref, join(b, a), 0, 1)


def next_kernel(parcel_ref, cols_ref, rows_ref, state_ref):
    for direction, state in enumerate(states((parcel_ref,), cols_ref[...], rows_ref)[0]):
        put(state_ref, state, direction)


def slab_totals(me_ref, directions, inner_ref, straight, across):
    me = me_ref[0]
    first = me % 2 == 0
    lower = me // 2 % 2 == 0
    result = []
    for forward, chip, near, far in zip(directions, inner_ref, straight, across):
        beside = join_ordered(first == forward, near, far)
        result.append((join_ordered(lower == forward, chip, beside), beside))
    return result


def urgent_slab_kernel(me_ref, inner_ref, straight_ref, across_ref, cols_ref, rows_ref, urgent_ref):
    forward = me_ref[0] // 8 % 2 == 0
    straight = pick(forward, planes(straight_ref, 0), planes(straight_ref, 1))
    across = pick(forward, *states((across_ref,), cols_ref[...], rows_ref)[0])
    inner = pick(forward, planes(inner_ref, 1, 0), planes(inner_ref, 0, 1))
    ((total, _),) = slab_totals(me_ref, (forward,), (inner,), (straight,), (across,))
    put(urgent_ref, total)


def slab_kernel(me_ref, inner_ref, straight_ref, across_ref, cols_ref, rows_ref, other_ref, outer_ref):
    me = me_ref[0]
    lower = me // 2 % 2 == 0
    forward = me // 8 % 2 == 0
    straight = planes(straight_ref, 0), planes(straight_ref, 1)
    across = states((across_ref,), cols_ref[...], rows_ref)[0]
    inner = planes(inner_ref, 1, 0), planes(inner_ref, 0, 1)
    fwd, bwd = slab_totals(me_ref, (True, False), inner, straight, across)
    ident = identity(fwd[0][0].shape)
    put(outer_ref, pick(lower, ident, fwd[1]), 0)
    put(outer_ref, pick(lower, bwd[1], ident), 1)
    put(other_ref, pick(forward, bwd[0], fwd[0]))


def level_kernel(level, me_ref, urgent_ref, other_ref, outer_ref, got_urgent_ref, got_other_ref, *out_refs):
    next_urgent_ref, next_other_ref, next_outer_ref = out_refs
    slab = me_ref[0] // 4
    lower = slab // 2**level % 2 == 0
    forward = slab // 2 ** (level + 1) % 2 == 0
    urgent, other = planes(urgent_ref), planes(other_ref)
    got_urgent, got_other = planes(got_urgent_ref), planes(got_other_ref)
    fwd, bwd = pick(forward, urgent, other), pick(forward, other, urgent)
    got_fwd, got_bwd = pick(forward, got_urgent, got_other), pick(forward, got_other, got_urgent)
    outer_fwd, outer_bwd = planes(outer_ref, 0), planes(outer_ref, 1)
    put(next_outer_ref, pick(lower, outer_fwd, join(got_fwd, outer_fwd)), 0)
    put(next_outer_ref, pick(lower, join(got_bwd, outer_bwd), outer_bwd), 1)
    fwd, bwd = join_ordered(lower, fwd, got_fwd), join_ordered(lower, got_bwd, bwd)
    forward = slab // 2 ** (level + 2) % 2 == 0
    put(next_urgent_ref, pick(forward, fwd, bwd))
    put(next_other_ref, pick(forward, bwd, fwd))


def urgent_kernel(level, me_ref, urgent_ref, got_ref, out_ref):
    slab = me_ref[0] // 4
    lower = slab // 2**level % 2 == 0
    forward = slab // 2 ** (level + 1) % 2 == 0
    put(out_ref, join_ordered(lower == forward, planes(urgent_ref), planes(got_ref)))


def gather_kernel(level, me_ref, inner_ref, outer_ref, urgent_ref, other_ref, known_ref):
    me = me_ref[0]
    slab = me // 4
    lower = slab // 2**level % 2 == 0
    forward = slab // 2 ** (level + 1) % 2 == 0
    near = pick(lower == forward, planes(other_ref), planes(urgent_ref))
    before, after = planes(outer_ref, 0), planes(outer_ref, 1)
    before = pick(lower, before, join(near, before))
    after = pick(lower, join(near, after), after)
    for flip in range(2):
        window = me % 2 ^ flip
        put(known_ref, join(before, planes(inner_ref, window, 0)), flip, 0)
        put(known_ref, join(after, planes(inner_ref, window, 1)), flip, 1)


def finish(state, out_ref):
    deep = out_ref.shape[2] // 2
    for k, plane in enumerate(strain(state) + state[4:]):
        for piece in range(out_ref.shape[1]):
            lanes = slice(piece * LANES, (piece + 1) * LANES)
            out_ref[k, piece, pl.ds(0, deep, stride=2), :] = plane[:deep, lanes]
            out_ref[k, piece, pl.ds(1, deep, stride=2), :] = plane[deep:, lanes]


def complete(forward, known_ref, last_ref, flip):
    fwd, bwd = planes(known_ref, flip, 0), planes(known_ref, flip, 1)
    return join(planes(last_ref), pick(forward, bwd, fwd))


def place(jobs, sems):
    copies = []
    for source, side, out_refs in jobs:
        pieces = source.shape[1]
        for piece in range(pieces):
            at = pl.multiple_of((side * pieces + piece) * LANES, LANES)
            start = 0
            for ref in out_refs:
                many = ref.shape[1]
                target = ref.at[0, :, :, pl.ds(at, LANES)]
                copies.append(
                    pltpu.make_async_copy(source.at[start : start + many, piece], target, sems.at[len(copies)])
                )
                start += many
    for copy in copies:
        copy.start()
    for copy in copies:
        copy.wait()


def is_forward(level, me_ref):
    return me_ref[0] // 4 // 2 ** (level + 1) % 2 == 0


def early_kernel(level, me_ref, known_ref, mine_ref, theirs_ref):
    forward = is_forward(level, me_ref)
    for flip, ref in enumerate((mine_ref, theirs_ref)):
        finish(pick(forward, planes(known_ref, flip, 0), planes(known_ref, flip, 1)), ref)


def theirs_kernel(level, me_ref, known_ref, last_ref, theirs_ref):
    finish(complete(is_forward(level, me_ref), known_ref, last_ref, 1), theirs_ref)


def mine_kernel(level, me_ref, known_ref, last_ref, early_ref, early_theirs_ref, *refs):
    *out_refs, mine_ref, sems = refs
    forward = is_forward(level, me_ref)
    core = me_ref[0] % 2
    finish(complete(forward, known_ref, last_ref, 0), mine_ref)
    for flag, early, late in ((forward, 0, 1), (jnp.logical_not(forward), 1, 0)):

        @pl.when(flag)
        def _():
            place(
                [
                    (early_ref, core, out_refs[early::2]),
                    (early_theirs_ref, 1 - core, out_refs[early::2]),
                    (mine_ref, core, out_refs[late::2]),
                ],
                sems,
            )


def place_kernel(level, me_ref, theirs_ref, *refs):
    *out_refs, sems = refs[4:]
    forward = is_forward(level, me_ref)
    for flag, late in ((forward, 1), (jnp.logical_not(forward), 0)):

        @pl.when(flag)
        def _():
            place([(theirs_ref, 1 - me_ref[0] % 2, out_refs[late::2])], sems)


SMEM = pl.BlockSpec(memory_space=pltpu.SMEM)
VMEM = pl.BlockSpec(memory_space=pltpu.VMEM)
HBM = pl.BlockSpec(memory_space=pltpu.HBM)
PARAMS = pltpu.CompilerParams(vmem_limit_bytes=8 * 1024 * 1024)


def sds(*shape, dtype=F32):
    return jax.ShapeDtypeStruct(shape, dtype)


def call(kernel, outs, *args, specs=None, out_specs=None, scratch=(), aliases=None):
    specs = specs or [SMEM] * (args[0].ndim == 1) + [VMEM] * (len(args) - (args[0].ndim == 1))
    many = isinstance(outs, tuple)
    out_specs = out_specs or ((VMEM,) * len(outs) if many else VMEM)
    return pl.pallas_call(
        kernel,
        out_shape=outs,
        in_specs=specs,
        out_specs=out_specs,
        scratch_shapes=scratch,
        input_output_aliases=aliases or {},
        compiler_params=PARAMS,
    )(*args)


def shards(velocity, substep_count, sea_mask, *, windows):
    rows, cols = sea_mask.shape
    half = cols // 2
    slabs = windows // 4
    last_level = slabs.bit_length() - 2
    me = lax.axis_index("tm").astype(jnp.int32)[None]

    def swap(x, d, keep=lambda i: True):
        return lax.ppermute(x, "tm", [(i, i ^ d) for i in range(windows) if keep(i)])

    tall = 4 * rows * (half // LANES) + TILE
    near, far = call(
        advance_kernel,
        (sds(tall, LANES), sds(tall, LANES)),
        me,
        substep_count, *(pltpu.with_memory_space_constraint(x, pltpu.HBM) for x in (velocity, sea_mask)),
        specs=[SMEM, SMEM, HBM, HBM],
        scratch=[
            pltpu.VMEM(velocity.shape, velocity.dtype),
            pltpu.VMEM(sea_mask.shape, sea_mask.dtype),
            pltpu.VMEM((*velocity.shape[1:3], cols // LANES, rows, LANES), F32),
            pltpu.SemaphoreType.DMA((2 + velocity.shape[1],)),
        ],
    )
    straight = swap(near, 2)
    across = swap(far, 3)
    next_core = swap(far, 1)
    one, both = sds(6, rows, half), sds(2, 6, rows, half)
    inner, col_table, row_table = call(
        chip_kernel,
        (
            sds(2, 2, 6, rows, half),
            sds(half + LANES, cols, dtype=BF16),
            sds(2, 4 * rows, 8 * rows, dtype=BF16),
        ),
        me,
        near,
        next_core,
    )
    straight = call(next_kernel, both, straight, col_table, row_table)
    urgent = call(urgent_slab_kernel, one, me, inner, straight, across, col_table, row_table)
    other, outer = call(slab_kernel, (one, both), me, inner, straight, across, col_table, row_table)
    for level in range(last_level - 1):
        urgent, other, outer = call(
            functools.partial(level_kernel, level),
            (one, one, both),
            me,
            urgent,
            other,
            outer,
            swap(urgent, 4 << level),
            swap(other, 4 << level),
        )
    level = last_level - 1

    def sends_other(i):
        return (i // 4 >> level) % 2 != (i // 4 >> last_level) % 2

    got_urgent = swap(urgent, 4 << level)
    got_other = swap(other, 4 << level)
    urgent = call(functools.partial(urgent_kernel, level), one, me, urgent, got_urgent)
    last = swap(urgent, 4 << last_level)
    known = call(
        functools.partial(gather_kernel, level), sds(2, 2, 6, rows, half), me, inner, outer, got_urgent, got_other
    )
    five = sds(5, half // LANES, rows, LANES)
    outs = (sds(1, 3, rows, cols), sds(1, 3, rows, cols), sds(1, 2, rows, cols), sds(1, 2, rows, cols))
    early, early_theirs = call(functools.partial(early_kernel, level), (five, five), me, known)
    early_theirs = swap(early_theirs, 1)
    theirs = swap(call(functools.partial(theirs_kernel, level), five, me, known, last), 1)
    most = call(
        functools.partial(mine_kernel, level),
        outs,
        me,
        known,
        last,
        early,
        early_theirs,
        out_specs=(HBM,) * 4,
        scratch=[pltpu.VMEM(five.shape, F32), pltpu.SemaphoreType.DMA((6 * (half // LANES),))],
    )
    return call(
        functools.partial(place_kernel, level),
        outs,
        me,
        theirs,
        *most,
        specs=[SMEM, VMEM] + [HBM] * 4,
        out_specs=(HBM,) * 4,
        scratch=[pltpu.SemaphoreType.DMA((2 * (half // LANES),))],
        aliases={2 + k: k for k in range(4)},
    )


def solution(mesh):
    return jax.shard_map(
        functools.partial(shards, windows=mesh.shape["tm"]),
        mesh=mesh,
        in_specs=(P("tm", None, None, "groups", None), P("tm"), P("groups", None)),
        out_specs=(P("tm", None, "groups", None),) * 4,
        check_vma=False,
    )
```
